128 devices in a mesh: gx: 8 (over x, z_hi), gy: 16 (over z_lo, y, core).
Axes of the slice: x: 4, y: 4, z: 4 (z_hi: 2, z_lo: 2; z = z_hi * 2 + z_lo), core: 2. Of those that a mesh axis runs over, the one named last changes fastest.
Arguments:
- hidden: bfloat16 [8192, 5376], P('gy', 'gx'), may hold values from -6 to 6
- start: int32 [1], replicated, may hold values from 1024 to 8191
- w_query: bfloat16 [5376, 4096], P('gx', 'gy'), may hold values from -0.078125 to 0.078125
- w_key_value: bfloat16 [5376, 2, 2048], P('gx', None, 'gy'), may hold values from -0.078125 to 0.078125
- w_out: bfloat16 [4096, 5376], P('gy', 'gx'), may hold values from -4 to 4
- cache: bfloat16 [1024, 2, 2048], P(None, None, 'gy'), may hold values from -6 to 6
Outputs:
- attn_branch: bfloat16 [8192, 5376], P('gy', 'gx')
The draws below stay inside these ranges and needn't reach their ends.
All inputs are finite; a program needn't handle non-finite values.
Results may differ from the reference program's by a relative error of at most 0.035.
Values may be sent and summed in bfloat16 or wider, within the bound.
No kernel may reach another device: no remote copies, remote signals or barrier semaphores. Data moves between devices by JAX's collectives and lax.ppermute only.
A program may use at most 192 MiB of HBM per device.

```python
import jax
import jax.numpy as jnp
from jax import lax

D = 5376
H = 32
KVH = 16
HD = 128
WINDOW = 1024
BLOCK = 1024
TOKENS = 8192
N_GX = 8
N_GY = 16


def shard_levels(stream_key, extent, cuts, least, high):
    def one(position, blocks):
        heights = jax.random.uniform(jax.random.fold_in(jax.random.fold_in(stream_key, 6), position), (blocks,), jnp.float32, least / len(cuts), high / len(cuts))
        return jnp.repeat(jnp.exp(heights), extent[position] // blocks).reshape((-1,) + (1,) * (len(extent) - position - 1))

    level = one(*cuts[0])
    for cut in cuts[1:]:
        level = level * one(*cut)
    return level


def scatter_about(key, shape, scale, bound, split=(), kind=jnp.bfloat16):
    values = jax.random.normal(key, shape, jnp.float32) * scale
    if len(split) > 0:
        values = shard_levels(key, shape, split, -0.22, 0.18) * values
    return jnp.clip(values, min=-bound, max=bound).astype(kind)


def setup_inputs(seed: int = 0) -> dict:
    seeds = jax.random.split(jax.random.key(seed), 7)
    return {
        "hidden": scatter_about(seeds[0], (TOKENS, D), 1.0, 6.0, ((0, 16), (1, 8))),
        "start": jax.random.randint(seeds[1], (1,), WINDOW, 8192).astype(jnp.int32),
        "w_query": scatter_about(seeds[2], (D, H * HD), D ** -0.5, 0.078125, ((0, 8), (1, 16))),
        "w_key_value": scatter_about(seeds[3], (D, 2, KVH * HD), D ** -0.5, 0.078125, ((0, 8), (2, 16))),
        "w_out": scatter_about(seeds[4], (H * HD, D), 0.3, 4.0, ((0, 16), (1, 8))),
        "cache": scatter_about(seeds[5], (WINDOW, 2, KVH * HD), 1.0, 6.0, ((2, 16),)),
    }


query_scale = 168.0 ** (-0.5)
norm_eps = 1e-06

def unit_rms(values):
    return values * lax.rsqrt(lax.optimization_barrier(jnp.mean(values * values, axis=-1, keepdims=True)) + norm_eps)

def rotate(values, positions):
    head_size = values.shape[-1]
    half_size = head_size // 2
    frequency = 10000.0 ** (-(2.0 * jnp.arange(half_size, dtype=jnp.float32)) / head_size)
    angles = positions.astype(jnp.float32)[:, None] * frequency[None, :]
    cosine = jnp.cos(angles)[:, None, :]
    sine_part = jnp.sin(angles)[:, None, :]
    first_half = values[..., :half_size]
    second = values[..., half_size:]
    return jnp.concatenate([first_half * cosine - second * sine_part, second * cosine + first_half * sine_part], axis=-1)

def attend(queries, query_pos, key_vals, key_pos):
    queries, key_vals = lax.optimization_barrier((queries, key_vals))
    query_wide = queries.astype(jnp.float32)
    kv_wide = key_vals.astype(jnp.float32)
    scores = jnp.einsum('qkgd,skd->qkgs', query_wide, kv_wide[:, 0])
    position_gap = query_pos[:, None] - key_pos[None, :]
    inside = (position_gap >= 0) & (position_gap < WINDOW)
    weights = jnp.where(inside[:, None, None, :], jnp.exp(scores), 0.0)
    denominator = lax.optimization_barrier(jnp.sum(weights, axis=-1))
    rounded = lax.optimization_barrier(weights.astype(jnp.bfloat16))
    summed = jnp.einsum('qkgs,skd->qkgd', rounded.astype(jnp.float32), kv_wide[:, 1])
    return (summed, denominator)

def reference(hidden, start, w_query, w_key_value, w_out, cache):
    slice_width = D // N_GX
    group_size = H // KVH
    columns = jnp.concatenate([w_query, w_key_value.reshape(D, 2 * KVH * HD)], axis=1)
    total_cols = columns.shape[1]
    hidden_parts = hidden.reshape(TOKENS, N_GX, slice_width)
    column_parts = columns.reshape(N_GX, slice_width, total_cols)

    def add_slice(running_sum, part_index):
        partial_value = jnp.dot(hidden_parts[:, part_index, :], column_parts[part_index], preferred_element_type=jnp.float32)
        rounded = lax.optimization_barrier(partial_value.astype(jnp.bfloat16))
        return (running_sum + rounded.astype(jnp.float32), None)
    summed_cols, unused = lax.scan(add_slice, jnp.zeros((TOKENS, total_cols), jnp.float32), jnp.arange(N_GX, dtype=jnp.int32))
    projected = summed_cols.astype(jnp.bfloat16)
    positions = start[0] + jnp.arange(TOKENS, dtype=jnp.int32)
    query_heads = projected[:, :H * HD].reshape(TOKENS, H, HD).astype(jnp.float32)
    queries = (rotate(unit_rms(query_heads), positions) * query_scale).astype(jnp.bfloat16)
    queries = queries.reshape(TOKENS, KVH, group_size, HD)
    kv_pairs = projected[:, H * HD:].reshape(TOKENS, 2, KVH, HD)
    key_part = rotate(unit_rms(kv_pairs[:, 0].astype(jnp.float32)), positions).astype(jnp.bfloat16)
    new_kv = jnp.stack([key_part, kv_pairs[:, 1]], axis=1)
    joined = jnp.concatenate([cache.reshape(WINDOW, 2, KVH, HD), new_kv], axis=0)
    joined_pos = start[0] - WINDOW + jnp.arange(WINDOW + TOKENS, dtype=jnp.int32)

    def one_block(block_index):
        row_start = (block_index * BLOCK).astype(jnp.int32)
        query_block = lax.dynamic_slice_in_dim(queries, row_start, BLOCK, 0)
        query_pos = lax.dynamic_slice_in_dim(positions, row_start, BLOCK, 0)
        context = lax.dynamic_slice_in_dim(joined, row_start, WINDOW + BLOCK, 0)
        context_pos = lax.dynamic_slice_in_dim(joined_pos, row_start, WINDOW + BLOCK, 0)
        summed, denominator = attend(query_block, query_pos, context, context_pos)
        return (summed / denominator[..., None]).reshape(BLOCK, H * HD).astype(jnp.bfloat16)
    mixed = lax.map(one_block, jnp.arange(N_GX, dtype=jnp.int32)).reshape(TOKENS, H * HD)
    group_cols = H // N_GY * HD
    mixed_parts = mixed.reshape(TOKENS, N_GY, group_cols)
    out_parts = w_out.reshape(N_GY, group_cols, D)

    def add_group(running_sum, part_index):
        partial_value = jnp.dot(mixed_parts[:, part_index, :], out_parts[part_index], preferred_element_type=jnp.float32)
        rounded = lax.optimization_barrier(partial_value.astype(jnp.bfloat16))
        return (running_sum + rounded.astype(jnp.float32), None)
    out_sum, unused = lax.scan(add_group, jnp.zeros((TOKENS, D), jnp.float32), jnp.arange(N_GY, dtype=jnp.int32))
    return out_sum.astype(jnp.bfloat16)
```

```python
import functools

import jax
import jax.numpy as jnp
from jax import lax
from jax.experimental import pallas as pl
from jax.experimental.pallas import tpu as pltpu
from jax.sharding import PartitionSpec as P

HD = 128
AXES = ("gx", "gy")
MIB = 1024 * 1024

query_scale = 168.0 ** (-0.5)
norm_eps = 1e-06


def place(index):
    gx, gy = divmod(index, 16)
    x, zh = divmod(gx, 2)
    zl, rest = divmod(gy, 8)
    y, core = divmod(rest, 2)
    return x, zh, zl, y, core


def number(x, zh, zl, y, core):
    return ((x % 4) * 2 + zh) * 16 + zl * 8 + (y % 4) * 2 + core


def move(value, to):
    return lax.ppermute(value, AXES, [(i, number(*to(*place(i)))) for i in range(128)])


def shift_x(value, by):
    return move(value, lambda x, zh, zl, y, c: (x + by, zh, zl, y, c))


def shift_y(value, by):
    return move(value, lambda x, zh, zl, y, c: (x, zh, zl, y + by, c))


def swap_zh(value):
    return move(value, lambda x, zh, zl, y, c: (x, 1 - zh, zl, y, c))


def swap_zl(value):
    return move(value, lambda x, zh, zl, y, c: (x, zh, 1 - zl, y, c))


def swap_core(value):
    return move(value, lambda x, zh, zl, y, c: (x, zh, zl, y, 1 - c))


def shear_y(value):
    return move(value, lambda x, zh, zl, y, c: (x, zh, zl, y + x, c))


def turn_x(value):
    return move(value, lambda x, zh, zl, y, c: (y - x, zl, zh, y, c))


def together(*values):
    return lax.optimization_barrier(values)


OFFSETS = ((0, 0), (0, 1), (3, 0), (1, 0), (3, 1), (1, 1), (2, 0), (2, 1))


def dot_first(a, b):
    return lax.dot_general(a, b, (((0,), (0,)), ((), ())), preferred_element_type=jnp.float32)


def dot_last(a, b):
    return lax.dot_general(a, b, (((1,), (1,)), ((), ())), preferred_element_type=jnp.float32)


def index_of(ring, pair):
    ring, pair = lax.rem(ring + 8, 4), lax.rem(pair, 2)
    base = jnp.where(ring == 0, 0, jnp.where(ring == 3, 2, jnp.where(ring == 1, 3, 6)))
    step = jnp.where((ring == 0) | (ring == 2), 1, 2)
    return base + step * pair


def coordinates():
    gx, gy = lax.axis_index("gx"), lax.axis_index("gy")
    zl, rest = lax.div(gy, 8), lax.rem(gy, 8)
    return lax.div(gx, 2), lax.rem(gx, 2), zl, lax.div(rest, 2), lax.rem(rest, 2)


def out_slots():
    x, zh, zl, y, core = coordinates()
    return [index_of(y + d - x, zl + e + zh) for d, e in OFFSETS]


def hidden_slots():
    x, zh, zl, y, core = coordinates()
    return [index_of(2 * x + d - y, zh + e + zl) for d, e in OFFSETS]


def load(blocks, held, sems):
    depth = blocks[0].shape[0]
    copies = [
        pltpu.make_async_copy(block, held.at[pl.ds(i * depth, depth)], sems.at[i])
        for i, block in enumerate(blocks)
    ]
    for copy in copies:
        copy.start()
    for copy in copies:
        copy.wait()


def add_products(own, other, slots, first, count, held_w, total):
    width, rows = own[0].shape
    for j in range(8):

        @pl.when((slots[j] >= first) & (slots[j] < first + count))
        def _():
            at = pl.ds(pl.multiple_of((slots[j] - first) * width, 16), width)
            for half, blocks in enumerate((own, other)):
                total[half] += dot_first(blocks[j][...], held_w[at, :])


def project_most_kernel(*refs):
    own, other, weights = refs[0:8], refs[8:16], refs[16:22]
    total, held_w, sems = refs[22:]
    load(weights, held_w, sems)
    total[...] = jnp.zeros_like(total)
    add_products(own, other, hidden_slots(), 0, 6, held_w, total)


def project_rest_kernel(*refs):
    own, other, weights = refs[0:8], refs[8:16], refs[16:18]
    before, cosine, sine, kv_out, q_out, total, held_w, sems = refs[18:]
    rows = own[0].shape[1]
    x, zh, zl, y, core = coordinates()
    load(weights, held_w, sems)
    total[...] = before[...]
    add_products(own, other, hidden_slots(), 6, 2, held_w, total)
    for half in range(2):
        for part in range(rows // 256):
            values = total[half, part * 256 : (part + 1) * 256, :].astype(jnp.bfloat16)
            wide = values.astype(jnp.float32)
            begin = (core if half == 0 else 1 - core) * rows + part * 256
            at = pl.ds(pl.multiple_of(begin, 256), 256)
            cos, sin = cosine[at, :], sine[at, :]

            def turned(v):
                v = v * lax.rsqrt(jnp.mean(v * v, axis=-1, keepdims=True) + norm_eps)
                return v * cos + pltpu.roll(v, HD // 2, 1) * sin

            kv_out[at, 0:HD] = turned(wide[:, 0:HD]).astype(jnp.bfloat16)
            kv_out[at, HD : 2 * HD] = values[:, HD : 2 * HD]
            for h in range(2):
                q = turned(wide[:, (2 + h) * HD : (3 + h) * HD]) * query_scale
                q_out[at, h * HD : (h + 1) * HD] = q.astype(jnp.bfloat16)


ANY_SPEC = pl.BlockSpec(memory_space=pl.ANY)
VMEM_SPEC = pl.BlockSpec(memory_space=pltpu.VMEM)


def project_most(own, other, weights):
    width, rows = own[0].shape
    columns = weights[0].shape[1]
    return pl.pallas_call(
        project_most_kernel,
        out_shape=jax.ShapeDtypeStruct((2, rows, columns), jnp.float32),
        in_specs=[VMEM_SPEC] * 16 + [ANY_SPEC] * 6,
        out_specs=VMEM_SPEC,
        scratch_shapes=[
            pltpu.VMEM((6 * width, columns), jnp.bfloat16),
            pltpu.SemaphoreType.DMA((6,)),
        ],
        compiler_params=pltpu.CompilerParams(vmem_limit_bytes=24 * MIB),
        cost_estimate=pl.CostEstimate(
            flops=4 * rows * 6 * width * columns, bytes_accessed=18 * MIB, transcendentals=0
        ),
        name="project_most",
    )(*own, *other, *weights)


def project_rest(own, other, weights, total, cosine, sine):
    width, rows = own[0].shape
    columns = weights[0].shape[1]
    shape = jax.ShapeDtypeStruct((2 * rows, 2 * HD), jnp.bfloat16)
    return pl.pallas_call(
        project_rest_kernel,
        out_shape=(shape, shape),
        in_specs=[VMEM_SPEC] * 16 + [ANY_SPEC] * 2 + [VMEM_SPEC] * 3,
        out_specs=(VMEM_SPEC, VMEM_SPEC),
        scratch_shapes=[
            pltpu.VMEM((2, rows, columns), jnp.float32),
            pltpu.VMEM((2 * width, columns), jnp.bfloat16),
            pltpu.SemaphoreType.DMA((2,)),
        ],
        compiler_params=pltpu.CompilerParams(vmem_limit_bytes=24 * MIB),
        cost_estimate=pl.CostEstimate(
            flops=4 * rows * 2 * width * columns, bytes_accessed=6 * MIB, transcendentals=0
        ),
        name="project_rest",
    )(*own, *other, *weights, total, cosine, sine)


def stacked(q_ref, begin, size):
    rows = pl.ds(begin, size)
    return jnp.concatenate([q_ref[rows, 0:HD], q_ref[rows, HD : 2 * HD]], axis=0)


QB = 256


def inside(size, keys, low):
    row = lax.broadcasted_iota(jnp.int32, (size, keys), 0)
    column = lax.broadcasted_iota(jnp.int32, (size, keys), 1)
    keep = column <= row if low else column > row
    return jnp.concatenate([keep, keep], axis=0)


def window(q_ref, kv_ref, i, low):
    count = q_ref.shape[0] // QB
    first, last = (0, i + 1) if low else (i, count)
    query = stacked(q_ref, i * QB, QB)
    total, weight = None, None
    for j in range(first, last):
        at = pl.ds(j * QB, QB)
        e = jnp.exp(dot_last(query, kv_ref[at, 0:HD]))
        if j == i:
            e = jnp.where(inside(QB, QB, low), e, 0.0)
        w = jnp.sum(e, axis=1, keepdims=True)
        t = jnp.dot(
            e.astype(jnp.bfloat16), kv_ref[at, HD : 2 * HD], preferred_element_type=jnp.float32
        )
        total = t if total is None else total + t
        weight = w if weight is None else weight + w
    return total, weight


def own_kernel(q_ref, kv_ref, total_ref, weight_ref):
    for i in range(q_ref.shape[0] // QB):
        total, weight = window(q_ref, kv_ref, i, True)
        weight = jnp.broadcast_to(weight, total.shape)
        for h in range(2):
            part = slice(h * QB, (h + 1) * QB)
            total_ref[pl.ds(i * QB, QB), h * HD : (h + 1) * HD] = total[part]
            weight_ref[pl.ds(i * QB, QB), h * HD : (h + 1) * HD] = weight[part]


def before_kernel(q_ref, kv_ref, total_ref, weight_ref, mixed_ref):
    for i in range(q_ref.shape[0] // QB):
        total, weight = window(q_ref, kv_ref, i, False)
        total = total + stacked(total_ref, i * QB, QB)
        weight = jnp.broadcast_to(weight, total.shape) + stacked(weight_ref, i * QB, QB)
        mixed = (total / weight).astype(jnp.bfloat16)
        for h in range(2):
            mixed_ref[pl.ds(i * QB, QB), h * HD : (h + 1) * HD] = mixed[h * QB : (h + 1) * QB]


def attention_cost(rows):
    pairs = rows * rows * 5 // 4
    return pl.CostEstimate(
        flops=4 * pairs * HD, bytes_accessed=8 * rows * 2 * HD, transcendentals=pairs
    )


def attend_own(q, kv):
    shape = jax.ShapeDtypeStruct(q.shape, jnp.float32)
    return pl.pallas_call(
        own_kernel,
        out_shape=(shape, shape),
        compiler_params=pltpu.CompilerParams(vmem_limit_bytes=24 * MIB),
        cost_estimate=attention_cost(q.shape[0]),
        name="attend_own",
    )(q, kv)


def attend_before(q, kv, total, weight):
    return pl.pallas_call(
        before_kernel,
        out_shape=jax.ShapeDtypeStruct(q.shape, jnp.bfloat16),
        compiler_params=pltpu.CompilerParams(vmem_limit_bytes=24 * MIB),
        cost_estimate=attention_cost(q.shape[0]),
        name="attend_before",
    )(q, kv, total, weight)


def out_most_kernel(*refs):
    mixed, weights = refs[0:6], refs[6:14]
    total, held_m, held_w, sems = refs[14:]
    depth = mixed[0].shape[1]
    slots = out_slots()
    copies = []
    for i in range(8):
        to = held_w.at[:, pl.ds(pl.multiple_of(slots[i] * depth, depth), depth)]
        copies.append(pltpu.make_async_copy(weights[i], to, sems.at[8 + i]))
    for i in range(6):
        here = held_m.at[:, pl.ds(i * depth, depth)]
        copies.append(pltpu.make_async_copy(mixed[i], here, sems.at[i]))
    for copy in copies:
        copy.start()
    for copy in copies:
        copy.wait()
    rows = total.shape[2]
    for half in range(2):
        here = held_m[half * rows : (half + 1) * rows, :]
        total[half] = dot_last(held_w[:, 0 : 6 * depth], here)


def out_rest_kernel(flip, *refs):
    mixed, weights = refs[0:2], refs[2:10]
    total, out, held_m, held_w, sems = refs[10:]
    rows, depth = out.shape[1], mixed[0].shape[1]
    slots = out_slots()
    x, zh, zl, y, core = coordinates()
    half = 1 - core if flip else core
    at = pl.ds(pl.multiple_of(half * rows, rows), rows)
    copies = []
    for i in range(2):
        here = held_m.at[:, pl.ds(i * depth, depth)]
        copy = pltpu.make_async_copy(mixed[i].at[at], here, sems.at[i])
        copy.start()
        copies.append(copy)
        for j in range(8):

            @pl.when(slots[j] == 6 + i)
            def _():
                to = held_w.at[:, pl.ds(i * depth, depth)]
                pltpu.make_async_copy(weights[j], to, sems.at[2 + i]).start()

        to = held_w.at[:, pl.ds(i * depth, depth)]
        copies.append(pltpu.make_async_copy(weights[0], to, sems.at[2 + i]))
    for copy in copies:
        copy.wait()
    out[...] = (total[half] + dot_last(held_w[...], held_m[...])).astype(out.dtype)


def out_most(mixed, weights):
    width, depth = weights[0].shape
    rows = mixed[0].shape[0] // 2
    return pl.pallas_call(
        out_most_kernel,
        out_shape=jax.ShapeDtypeStruct((2, width, rows), jnp.float32),
        in_specs=[ANY_SPEC] * 14,
        out_specs=VMEM_SPEC,
        scratch_shapes=[
            pltpu.VMEM((2 * rows, 6 * depth), jnp.bfloat16),
            pltpu.VMEM((width, 8 * depth), jnp.bfloat16),
            pltpu.SemaphoreType.DMA((16,)),
        ],
        compiler_params=pltpu.CompilerParams(vmem_limit_bytes=24 * MIB),
        cost_estimate=pl.CostEstimate(
            flops=4 * rows * 6 * depth * width, bytes_accessed=8 * MIB, transcendentals=0
        ),
        name="out_most",
    )(*mixed, *weights)


def out_rest(mixed, weights, total, kind, flip):
    width, depth = weights[0].shape
    rows = mixed[0].shape[0] // 2
    return pl.pallas_call(
        functools.partial(out_rest_kernel, flip),
        out_shape=jax.ShapeDtypeStruct((width, rows), kind),
        in_specs=[ANY_SPEC] * 10 + [VMEM_SPEC],
        out_specs=VMEM_SPEC,
        scratch_shapes=[
            pltpu.VMEM((rows, 2 * depth), jnp.bfloat16),
            pltpu.VMEM((width, 2 * depth), jnp.bfloat16),
            pltpu.SemaphoreType.DMA((4,)),
        ],
        compiler_params=pltpu.CompilerParams(vmem_limit_bytes=20 * MIB),
        cost_estimate=pl.CostEstimate(
            flops=2 * rows * 2 * depth * width, bytes_accessed=4 * MIB, transcendentals=0
        ),
        name="out_rest",
    )(*mixed, *weights, total)


def shards(hidden, start, w_query, w_key_value, w_out, cache):
    rows, width = hidden.shape
    chip = lax.axis_index("gy") // 2

    positions = start[0] + chip * 2 * rows + jnp.arange(2 * rows, dtype=jnp.int32)
    half = HD // 2
    frequency = 10000.0 ** (-(2.0 * jnp.arange(half, dtype=jnp.float32)) / HD)
    angles = positions.astype(jnp.float32)[:, None] * frequency[None, :]
    cosine, sine = jnp.cos(angles), jnp.sin(angles)
    cosine = jnp.concatenate([cosine, cosine], axis=1)
    sine = jnp.concatenate([-sine, sine], axis=1)

    weight = jnp.concatenate([w_key_value.reshape(width, 2 * HD), w_query], axis=1)
    block = hidden.T
    out_block = w_out.T

    moved = shear_y(weight)
    block_z = swap_zh(block)
    block_r, block_l = shift_x(block, 1), shift_x(block, -1)
    moved, block_z, block_r, block_l, out_block, cache = together(
        moved, block_z, block_r, block_l, out_block, cache
    )
    moved = turn_x(moved)
    out_z, out_r, out_l = swap_zl(out_block), shift_y(out_block, 1), shift_y(out_block, -1)
    moved, block_z, out_z, out_r, out_l = together(moved, block_z, out_z, out_r, out_l)
    moved_z = swap_zl(moved)
    moved_r, moved_l = shift_y(moved, 1), shift_y(moved, -1)
    block_zr, block_zl = shift_x(block_z, 1), shift_x(block_z, -1)
    moved_z, moved_r, moved_l, block_zr, block_zl, block_r = together(
        moved_z, moved_r, moved_l, block_zr, block_zl, block_r
    )
    moved_zr, moved_zl = shift_y(moved_z, 1), shift_y(moved_z, -1)
    block_f, block_zf = shift_x(block_r, 1), shift_x(block_zl, -1)
    moved_zr, moved_zl, block_f, block_zf, out_z, out_l, cache = together(
        moved_zr, moved_zl, block_f, block_zf, out_z, out_l, cache
    )
    moved_f, moved_zf = shift_y(moved_r, 1), shift_y(moved_zl, -1)
    own = [block, block_z, block_r, block_l, block_zr, block_zl, block_f, block_zf]
    other = [swap_core(b) for b in own]
    pairs = []
    for gx in range(8):
        head = 8 * (gx % 2) + 2 * (gx // 2)
        pairs += [(gx * 16 + head + c, gx * 16 + c) for c in range(2)]
    cached = lax.ppermute(cache.reshape(2 * rows, 2 * HD), AXES, pairs)
    total = project_most(own, other, [moved, moved_z, moved_r, moved_l, moved_zr, moved_zl])
    kv, q = project_rest(own, other, [moved_f, moved_zf], total, cosine, sine)

    kv, q, out_z, out_r = together(kv, q, out_z, out_r)
    before = lax.ppermute(kv, "gy", [(i, i + 2) for i in range(14)])
    out_zr, out_zl = shift_y(out_z, 1), shift_y(out_z, -1)
    total, weight_sum = attend_own(q, kv)
    before = jnp.where(chip == 0, cached, before)
    mixed = attend_before(q, before, total, weight_sum)

    mixed, out_r, out_zr, out_zl = together(mixed, out_r, out_zr, out_zl)
    mixed_z = swap_zh(mixed)
    mixed_r, mixed_l = shift_x(mixed, 1), shift_x(mixed, -1)
    out_f, out_zf = shift_y(out_r, 1), shift_y(out_zl, -1)
    mixed_z, mixed_r, mixed_l = together(mixed_z, mixed_r, mixed_l)
    mixed_zr, mixed_zl = shift_x(mixed_z, 1), shift_x(mixed_z, -1)
    mixed_zr, mixed_zl, mixed_r = together(mixed_zr, mixed_zl, mixed_r)
    mixed_f, mixed_zf = shift_x(mixed_r, 1), shift_x(mixed_zl, -1)
    outs = [out_block, out_z, out_r, out_l, out_zr, out_zl, out_f, out_zf]
    total = out_most([mixed, mixed_z, mixed_r, mixed_l, mixed_zr, mixed_zl], outs)
    sent = swap_core(out_rest([mixed_f, mixed_zf], outs, total, jnp.bfloat16, True))
    kept = out_rest([mixed_f, mixed_zf], outs, total, jnp.float32, False)
    return (kept + sent.astype(jnp.float32)).astype(jnp.bfloat16).T


def solution(mesh):
    return jax.shard_map(
        shards,
        mesh=mesh,
        in_specs=(
            P("gy", "gx"),
            P(),
            P("gx", "gy"),
            P("gx", None, "gy"),
            P("gy", "gx"),
            P(None, None, "gy"),
        ),
        out_specs=P("gy", "gx"),
        check_vma=False,
    )
```

```python
import functools

import jax
import jax.numpy as jnp
import numpy as np
from jax import lax
from jax.experimental import pallas as pl
from jax.experimental.pallas import tpu as pltpu
from jax.sharding import PartitionSpec as P

HD = 128
AXES = ("gx", "gy")
MIB = 1024 * 1024

query_scale = 168.0 ** (-0.5)
norm_eps = 1e-06


def place(index):
    gx, gy = divmod(index, 16)
    x, zh = divmod(gx, 2)
    zl, rest = divmod(gy, 8)
    y, core = divmod(rest, 2)
    return x, zh, zl, y, core


def number(x, zh, zl, y, core):
    return ((x % 4) * 2 + zh) * 16 + zl * 8 + (y % 4) * 2 + core


def move(value, to):
    return lax.ppermute(value, AXES, [(i, number(*to(*place(i)))) for i in range(128)])


def shift_x(value, by):
    return move(value, lambda x, zh, zl, y, c: (x + by, zh, zl, y, c))


def shift_y(value, by):
    return move(value, lambda x, zh, zl, y, c: (x, zh, zl, y + by, c))


def swap_zh(value):
    return move(value, lambda x, zh, zl, y, c: (x, 1 - zh, zl, y, c))


def swap_zl(value):
    return move(value, lambda x, zh, zl, y, c: (x, zh, 1 - zl, y, c))


def swap_core(value):
    return move(value, lambda x, zh, zl, y, c: (x, zh, zl, y, 1 - c))


def shear_y(value):
    return move(value, lambda x, zh, zl, y, c: (x, zh, zl, y + x, c))


def turn_x(value):
    return move(value, lambda x, zh, zl, y, c: (y - x, zl, zh, y, c))


def together(*values):
    return lax.optimization_barrier(values)


OFFSETS = ((0, 0), (0, 1), (3, 0), (1, 0), (3, 1), (1, 1), (2, 0), (2, 1))


def index_of(ring, pair):
    ring, pair = lax.rem(ring + 8, 4), lax.rem(pair, 2)
    base = jnp.where(ring == 0, 0, jnp.where(ring == 3, 2, jnp.where(ring == 1, 3, 6)))
    step = jnp.where((ring == 0) | (ring == 2), 1, 2)
    return base + step * pair


def coordinates():
    gx, gy = lax.axis_index("gx"), lax.axis_index("gy")
    zl, rest = lax.div(gy, 8), lax.rem(gy, 8)
    return lax.div(gx, 2), lax.rem(gx, 2), zl, lax.div(rest, 2), lax.rem(rest, 2)


def out_slots():
    x, zh, zl, y, core = coordinates()
    return [index_of(y + d - x, zl + e + zh) for d, e in OFFSETS]


def hidden_slots():
    x, zh, zl, y, core = coordinates()
    return [index_of(2 * x + d - y, zh + e + zl) for d, e in OFFSETS]


def project_most_kernel(*refs):
    own, other, weights = refs[0:8], refs[8:16], refs[16:23]
    total, left, held_w, staged, sems = refs[23:]
    width, rows = own[0].shape
    slots = hidden_slots()
    copies = [
        pltpu.make_async_copy(block, staged.at[i], sems.at[i]) for i, block in enumerate(weights)
    ]
    for copy in copies:
        copy.start()
    total[...] = jnp.zeros_like(total)
    for i, copy in enumerate(copies):
        copy.wait()
        held_w[i] = staged[i].T
    for j in range(8):

        @pl.when(slots[j] < 7)
        def _():
            weight = held_w[slots[j]]
            for half, blocks in enumerate((own, other)):
                at = slice(half * rows, (half + 1) * rows)
                total[:, at] += jnp.dot(
                    weight, blocks[j][...], preferred_element_type=jnp.float32
                )

        @pl.when(slots[j] == 7)
        def _():
            left[:, 0:rows] = own[j][...]
            left[:, rows : 2 * rows] = other[j][...]


def turned(v, cos, sin):
    v = v * lax.rsqrt(jnp.mean(v * v, axis=0, keepdims=True) + norm_eps)
    swapped = jnp.concatenate([v[HD // 2 :], v[: HD // 2]], axis=0)
    return v * cos + swapped * sin


def places(rows):
    core = lax.rem(lax.axis_index("gy"), 2)
    for half in range(2):
        begin = pl.multiple_of((core if half == 0 else 1 - core) * rows, rows)
        yield slice(half * rows, (half + 1) * rows), pl.ds(begin, rows)


def finish(left, weight, before):
    return before + jnp.dot(weight[...].T, left[...], preferred_element_type=jnp.float32)


def project_kv_kernel(weight, q_weight, left, before, cosine, sine, kv_out):
    total = finish(left, weight, before[0 : 2 * HD, :])
    for here, at in places(left.shape[1] // 2):
        values = total[:, here].astype(jnp.bfloat16)
        key = turned(values[0:HD].astype(jnp.float32), cosine[:, at], sine[:, at])
        kv_out[0:HD, at] = key.astype(jnp.bfloat16)
        kv_out[HD : 2 * HD, at] = values[HD : 2 * HD]


def project_q_kernel(weight, kv, left, before, cosine, sine, q_out):
    total = finish(left, weight, before[2 * HD : 4 * HD, :])
    for here, at in places(left.shape[1] // 2):
        values = total[:, here].astype(jnp.bfloat16).astype(jnp.float32)
        for h in range(2):
            part = slice(h * HD, (h + 1) * HD)
            query = turned(values[part], cosine[:, at], sine[:, at]) * query_scale
            q_out[part, at] = query.astype(jnp.bfloat16)


LIGHT = pl.CostEstimate(flops=1024, bytes_accessed=1024, transcendentals=0)
ANY_SPEC = pl.BlockSpec(memory_space=pl.ANY)
VMEM_SPEC = pl.BlockSpec(memory_space=pltpu.VMEM)


def project_most(own, other, weights):
    width, rows = own[0].shape
    columns = weights[0].shape[1]
    return pl.pallas_call(
        project_most_kernel,
        out_shape=(
            jax.ShapeDtypeStruct((columns, 2 * rows), jnp.float32),
            jax.ShapeDtypeStruct((width, 2 * rows), jnp.bfloat16),
        ),
        in_specs=[VMEM_SPEC] * 16 + [ANY_SPEC] * 7,
        out_specs=(VMEM_SPEC, VMEM_SPEC),
        scratch_shapes=[
            pltpu.VMEM((7, columns, width), jnp.bfloat16),
            pltpu.VMEM((7, width, columns), jnp.bfloat16),
            pltpu.SemaphoreType.DMA((7,)),
        ],
        compiler_params=pltpu.CompilerParams(vmem_limit_bytes=26 * MIB),
        cost_estimate=pl.CostEstimate(
            flops=28 * rows * width * columns, bytes_accessed=30 * MIB, transcendentals=0
        ),
        name="project_most",
    )(*own, *other, *weights)


def project_rest(kernel, weight, after, left, total, cosine, sine):
    return pl.pallas_call(
        kernel,
        out_shape=jax.ShapeDtypeStruct((weight.shape[1], left.shape[1]), jnp.bfloat16),
        in_specs=[VMEM_SPEC, ANY_SPEC] + [VMEM_SPEC] * 4,
        out_specs=VMEM_SPEC,
        compiler_params=pltpu.CompilerParams(vmem_limit_bytes=20 * MIB),
        cost_estimate=LIGHT,
        name="project_rest",
    )(weight, after, left, total, cosine, sine)


def small_call(kernel, out_shape, *args, in_specs=None):
    return pl.pallas_call(
        kernel,
        out_shape=out_shape,
        in_specs=in_specs or [VMEM_SPEC] * len(args),
        out_specs=jax.tree.map(lambda _: VMEM_SPEC, out_shape),
        compiler_params=pltpu.CompilerParams(vmem_limit_bytes=8 * MIB),
        cost_estimate=LIGHT,
        name="small",
    )(*args)


def angles_kernel(start, frequency, cosine, sine):
    rows = cosine.shape[1]
    chip = lax.div(lax.axis_index("gy"), 2)
    column = lax.broadcasted_iota(jnp.int32, (HD // 2, rows), 1)
    positions = (start[0] + chip * rows + column).astype(jnp.float32)
    angles = positions * frequency[...]
    cos, sin = jnp.cos(angles), jnp.sin(angles)
    cosine[0 : HD // 2, :] = cos
    cosine[HD // 2 : HD, :] = cos
    sine[0 : HD // 2, :] = -sin
    sine[HD // 2 : HD, :] = sin


def angles_of(start, rows):
    frequency = 10000.0 ** (-2.0 * np.arange(HD // 2) / HD)
    frequency = jnp.asarray(np.repeat(frequency[:, None], rows, axis=1), jnp.float32)
    shape = jax.ShapeDtypeStruct((HD, rows), jnp.float32)
    specs = [pl.BlockSpec(memory_space=pltpu.SMEM), VMEM_SPEC]
    return small_call(angles_kernel, (shape, shape), start, frequency, in_specs=specs)


def beside_kernel(left, right, out):
    columns = left.shape[1]
    out[:, 0:columns] = left[...]
    out[:, columns : 2 * columns] = right[...]


def beside(left, right):
    rows, columns = left.shape
    shape = jax.ShapeDtypeStruct((rows, 2 * columns), left.dtype)
    return small_call(beside_kernel, shape, left, right)


def halves_kernel(first, second, low, high):
    columns = low.shape[1]
    low[...] = first[:, 0:columns]
    high[...] = second[:, columns : 2 * columns]


def halves(first, second):
    rows, columns = first.shape
    shape = jax.ShapeDtypeStruct((rows, columns // 2), first.dtype)
    return small_call(halves_kernel, (shape, shape), first, second)


QB = 256


def window(q_ref, kv_ref, keys, i, low):
    count = q_ref.shape[1] // QB
    first, last = (0, i + 1) if low else (i, count)
    at = pl.ds(i * QB, QB)
    query = jnp.concatenate([q_ref[0:HD, at], q_ref[HD : 2 * HD, at]], axis=1)
    total, weight = None, None
    for j in range(first, last):
        here = slice(j * QB, (j + 1) * QB)
        e = jnp.exp(jnp.dot(keys[here], query, preferred_element_type=jnp.float32))
        if j == i:
            key = lax.broadcasted_iota(jnp.int32, (QB, QB), 0)
            column = lax.broadcasted_iota(jnp.int32, (QB, QB), 1)
            keep = key <= column if low else key > column
            e = jnp.where(jnp.concatenate([keep, keep], axis=1), e, 0.0)
        w = jnp.sum(e, axis=0, keepdims=True)
        t = jnp.dot(
            kv_ref[HD : 2 * HD, here], e.astype(jnp.bfloat16), preferred_element_type=jnp.float32
        )
        total = t if total is None else total + t
        weight = w if weight is None else weight + w
    return total, weight


def own_kernel(q_ref, kv_ref, total_ref, weight_ref, keys):
    keys[...] = kv_ref[0:HD, :].T
    for i in range(q_ref.shape[1] // QB):
        total, weight = window(q_ref, kv_ref, keys, i, True)
        for h in range(2):
            part = slice(h * QB, (h + 1) * QB)
            at = pl.ds(i * QB, QB)
            total_ref[h * HD : (h + 1) * HD, at] = total[:, part]
            weight_ref[h : h + 1, at] = weight[:, part]


def before_kernel(q_ref, sent_ref, cached_ref, total_ref, weight_ref, mixed_ref, kv_ref, keys):
    chip = lax.div(lax.axis_index("gy"), 2)

    @pl.when(chip == 0)
    def _():
        kv_ref[...] = cached_ref[...]

    @pl.when(chip > 0)
    def _():
        kv_ref[...] = sent_ref[...]

    keys[...] = kv_ref[0:HD, :].T
    for i in range(q_ref.shape[1] // QB):
        total, weight = window(q_ref, kv_ref, keys, i, False)
        for h in range(2):
            part = slice(h * QB, (h + 1) * QB)
            at = pl.ds(i * QB, QB)
            row = slice(h * HD, (h + 1) * HD)
            top = total[:, part] + total_ref[row, at]
            low = weight[:, part] + weight_ref[h : h + 1, at]
            mixed_ref[row, at] = (top / low).astype(jnp.bfloat16)


def attend_own(q, kv):
    rows = q.shape[1]
    return pl.pallas_call(
        own_kernel,
        out_shape=(
            jax.ShapeDtypeStruct(q.shape, jnp.float32),
            jax.ShapeDtypeStruct((2, rows), jnp.float32),
        ),
        scratch_shapes=[pltpu.VMEM((rows, HD), jnp.bfloat16)],
        compiler_params=pltpu.CompilerParams(vmem_limit_bytes=20 * MIB),
        cost_estimate=LIGHT,
        name="attend_own",
    )(q, kv)


def attend_before(q, sent, cached, total, weight):
    rows = q.shape[1]
    return pl.pallas_call(
        before_kernel,
        out_shape=jax.ShapeDtypeStruct(q.shape, jnp.bfloat16),
        scratch_shapes=[
            pltpu.VMEM(sent.shape, jnp.bfloat16),
            pltpu.VMEM((rows, HD), jnp.bfloat16),
        ],
        compiler_params=pltpu.CompilerParams(vmem_limit_bytes=20 * MIB),
        cost_estimate=LIGHT,
        name="attend_before",
    )(q, sent, cached, total, weight)


def out_most_kernel(*refs):
    mixed, weights = refs[0:7], refs[7:15]
    total, left, held_m, held_w, sems = refs[15:]
    depth = mixed[0].shape[0]
    slots = out_slots()
    copies = []
    for i in range(8):
        to = held_w.at[:, pl.ds(pl.multiple_of(slots[i] * depth, depth), depth)]
        copies.append(pltpu.make_async_copy(weights[i], to, sems.at[8 + i]))
    for i in range(7):
        here = held_m.at[pl.ds(i * depth, depth), :]
        copies.append(pltpu.make_async_copy(mixed[i], here, sems.at[i]))
    for copy in copies:
        copy.start()
    for copy in copies:
        copy.wait()
    rows = total.shape[2]
    left[...] = held_w[:, 7 * depth : 8 * depth]
    for half in range(2):
        here = held_m[:, half * rows : (half + 1) * rows]
        total[half] = jnp.dot(
            held_w[:, 0 : 7 * depth], here, preferred_element_type=jnp.float32
        )


def out_rest_kernel(flip, left, low, high, total, out):
    core = lax.rem(lax.axis_index("gy"), 2)
    half = 1 - core if flip else core
    for side, mixed in enumerate((low, high)):

        @pl.when(half == side)
        def _():
            product = jnp.dot(left[...], mixed[...], preferred_element_type=jnp.float32)
            out[...] = (total[side] + product).astype(out.dtype)


def out_most(mixed, weights):
    width, depth = weights[0].shape
    rows = mixed[0].shape[1] // 2
    return pl.pallas_call(
        out_most_kernel,
        out_shape=(
            jax.ShapeDtypeStruct((2, width, rows), jnp.float32),
            jax.ShapeDtypeStruct((width, depth), jnp.bfloat16),
        ),
        in_specs=[ANY_SPEC] * 15,
        out_specs=(VMEM_SPEC, VMEM_SPEC),
        scratch_shapes=[
            pltpu.VMEM((7 * depth, 2 * rows), jnp.bfloat16),
            pltpu.VMEM((width, 8 * depth), jnp.bfloat16),
            pltpu.SemaphoreType.DMA((16,)),
        ],
        compiler_params=pltpu.CompilerParams(vmem_limit_bytes=20 * MIB),
        cost_estimate=LIGHT,
        name="out_most",
    )(*mixed, *weights)


def out_rest(left, low, high, total, kind, flip):
    return pl.pallas_call(
        functools.partial(out_rest_kernel, flip),
        out_shape=jax.ShapeDtypeStruct(total.shape[1:], kind),
        in_specs=[VMEM_SPEC] * 4,
        out_specs=VMEM_SPEC,
        compiler_params=pltpu.CompilerParams(vmem_limit_bytes=20 * MIB),
        cost_estimate=LIGHT,
        name="out_rest",
    )(left, low, high, total)


def shards(hidden, start, w_query, w_key_value, w_out, cache):
    rows, width = hidden.shape
    kv_weight = w_key_value.reshape(width, 2 * HD)
    kv_weight, hidden = together(kv_weight, hidden)
    block = hidden.T
    out_block = w_out.T

    moved_q, moved_kv = shear_y(w_query), shear_y(kv_weight)
    block_z = swap_zh(block)
    block_r, block_l = shift_x(block, 1), shift_x(block, -1)
    moved_q, moved_kv, block_z, block_r, block_l, out_block, cache = together(
        moved_q, moved_kv, block_z, block_r, block_l, out_block, cache
    )
    moved = beside(turn_x(moved_kv), turn_x(moved_q))
    out_z, out_r, out_l = swap_zl(out_block), shift_y(out_block, 1), shift_y(out_block, -1)
    other = [swap_core(block), swap_core(block_z)]
    cosine, sine = angles_of(start, 2 * rows)
    moved, block_z, out_z, out_r, out_l, cosine, sine, *other = together(
        moved, block_z, out_z, out_r, out_l, cosine, sine, *other
    )
    moved_z = swap_zl(moved)
    moved_r, moved_l = shift_y(moved, 1), shift_y(moved, -1)
    block_zr, block_zl = shift_x(block_z, 1), shift_x(block_z, -1)
    other += [swap_core(block_r), swap_core(block_l)]
    moved_z, moved_r, moved_l, block_zr, block_zl, block_r, *other = together(
        moved_z, moved_r, moved_l, block_zr, block_zl, block_r, *other
    )
    moved_f, moved_zl, moved_zr = shift_y(moved_r, 1), shift_y(moved_z, -1), swap_zl(moved_r)
    block_f, block_zf = shift_x(block_r, 1), shift_x(block_zl, -1)
    other += [swap_core(block_zr), swap_core(block_zl)]
    moved_f, moved_zr, moved_zl, block_f, block_zf, out_z, out_l, cache, *other = together(
        moved_f, moved_zr, moved_zl, block_f, block_zf, out_z, out_l, cache, *other
    )
    half_zl, half_zr = halves(moved_zl, moved_zr)
    last_kv, last_q = shift_y(half_zl, -1), shift_y(half_zr, 1)
    own = [block, block_z, block_r, block_l, block_zr, block_zl, block_f, block_zf]
    other += [swap_core(block_f), swap_core(block_zf)]
    pairs = []
    for gx in range(8):
        head = 8 * (gx % 2) + 2 * (gx // 2)
        pairs += [(gx * 16 + head + c, gx * 16 + c) for c in range(2)]
    cached = lax.ppermute(cache, AXES, pairs)
    total, left = project_most(own, other, [moved, moved_z, moved_r, moved_l, moved_zr, moved_zl, moved_f])
    kv = project_rest(project_kv_kernel, last_kv, last_q, left, total, cosine, sine)
    before = lax.ppermute(kv, "gy", [(i, i + 2) for i in range(14)])
    q = project_rest(project_q_kernel, last_q, kv, left, total, cosine, sine)

    kv, q, out_z, out_r, cached = together(kv, q, out_z, out_r, cached)
    cached = cached.reshape(2 * rows, 2 * HD).T
    out_zr, out_zl = shift_y(out_z, 1), shift_y(out_z, -1)
    total, weight_sum = attend_own(q, kv)
    mixed = attend_before(q, before, cached, total, weight_sum)

    mixed, out_r, out_zr, out_zl = together(mixed, out_r, out_zr, out_zl)
    mixed_z = swap_zh(mixed)
    mixed_r, mixed_l = shift_x(mixed, 1), shift_x(mixed, -1)
    out_f, out_zf = shift_y(out_r, 1), shift_y(out_zl, -1)
    mixed_z, mixed_r, mixed_l = together(mixed_z, mixed_r, mixed_l)
    mixed_f, mixed_zl, mixed_zr = shift_x(mixed_r, 1), shift_x(mixed_z, -1), swap_zh(mixed_r)
    mixed_f, mixed_zr, mixed_zl = together(mixed_f, mixed_zr, mixed_zl)
    low, high = halves(mixed_zr, mixed_zl)
    low, high = shift_x(low, 1), shift_x(high, -1)
    outs = [out_block, out_z, out_r, out_l, out_zr, out_zl, out_f, out_zf]
    gathered = [mixed, mixed_z, mixed_r, mixed_l, mixed_zr, mixed_zl, mixed_f]
    total, left = out_most(gathered, outs)
    sent = swap_core(out_rest(left, low, high, total, jnp.bfloat16, True))
    kept = out_rest(left, low, high, total, jnp.float32, False)
    return (kept + sent.astype(jnp.float32)).astype(jnp.bfloat16).T


def solution(mesh):
    return jax.shard_map(
        shards,
        mesh=mesh,
        in_specs=(
            P("gy", "gx"),
            P(),
            P("gx", "gy"),
            P("gx", None, "gy"),
            P("gy", "gx"),
            P(None, None, "gy"),
        ),
        out_specs=P("gy", "gx"),
        check_vma=False,
    )
```

```python
import functools

import jax
import jax.numpy as jnp
import numpy as np
from jax import lax
from jax.experimental import pallas as pl
from jax.experimental.pallas import tpu as pltpu
from jax.sharding import PartitionSpec as P

HD = 128
AXES = ("gx", "gy")
MIB = 1024 * 1024

query_scale = 168.0 ** (-0.5)
norm_eps = 1e-06


def place(index):
    gx, gy = divmod(index, 16)
    x, zh = divmod(gx, 2)
    zl, rest = divmod(gy, 8)
    y, core = divmod(rest, 2)
    return x, zh, zl, y, core


def number(x, zh, zl, y, core):
    return ((x % 4) * 2 + zh) * 16 + zl * 8 + (y % 4) * 2 + core


def move(value, to):
    return lax.ppermute(value, AXES, [(i, number(*to(*place(i)))) for i in range(128)])


def shift_x(value, by):
    return move(value, lambda x, zh, zl, y, c: (x + by, zh, zl, y, c))


def shift_y(value, by):
    return move(value, lambda x, zh, zl, y, c: (x, zh, zl, y + by, c))


def swap_zh(value):
    return move(value, lambda x, zh, zl, y, c: (x, 1 - zh, zl, y, c))


def swap_zl(value):
    return move(value, lambda x, zh, zl, y, c: (x, zh, 1 - zl, y, c))


def swap_core(value):
    return move(value, lambda x, zh, zl, y, c: (x, zh, zl, y, 1 - c))


def shear_y(value):
    return move(value, lambda x, zh, zl, y, c: (x, zh, zl, y + x, c))


def turn_x(value):
    return move(value, lambda x, zh, zl, y, c: (y - x, zl, zh, y, c))


def together(*values):
    return lax.optimization_barrier(values)


OFFSETS = ((0, 0), (0, 1), (3, 0), (1, 0), (3, 1), (1, 1), (2, 0), (2, 1))


def index_of(ring, pair):
    ring, pair = lax.rem(ring + 8, 4), lax.rem(pair, 2)
    base = jnp.where(ring == 0, 0, jnp.where(ring == 3, 2, jnp.where(ring == 1, 3, 6)))
    step = jnp.where((ring == 0) | (ring == 2), 1, 2)
    return base + step * pair


def coordinates():
    gx, gy = lax.axis_index("gx"), lax.axis_index("gy")
    zl, rest = lax.div(gy, 8), lax.rem(gy, 8)
    return lax.div(gx, 2), lax.rem(gx, 2), zl, lax.div(rest, 2), lax.rem(rest, 2)


def out_slots():
    x, zh, zl, y, core = coordinates()
    return [index_of(y + d - x, zl + e + zh) for d, e in OFFSETS]


def hidden_slots():
    x, zh, zl, y, core = coordinates()
    return [index_of(2 * x + d - y, zh + e + zl) for d, e in OFFSETS]


def turn_kernel(*refs):
    blocks, out = refs[:-1], refs[-1]
    for i, block in enumerate(blocks):
        out[i] = block[...].T


def turn(blocks):
    width, columns = blocks[0].shape
    shape = jax.ShapeDtypeStruct((len(blocks), columns, width), blocks[0].dtype)
    return small_call(turn_kernel, shape, *blocks)


def project_most_kernel(*refs):
    blocks, early, late, total, left = refs[0:8], refs[8], refs[9], refs[10], refs[11]
    slots = hidden_slots()
    total[...] = jnp.zeros_like(total)
    for j in range(8):

        @pl.when(slots[j] < 4)
        def _():
            weight = early[jnp.minimum(slots[j], 3)]
            total[...] += jnp.dot(weight, blocks[j][...], preferred_element_type=jnp.float32)

        @pl.when((slots[j] >= 4) & (slots[j] < 7))
        def _():
            weight = late[jnp.clip(slots[j] - 4, 0, 2)]
            total[...] += jnp.dot(weight, blocks[j][...], preferred_element_type=jnp.float32)

        @pl.when(slots[j] == 7)
        def _():
            left[...] = blocks[j][...]


def turned(v, cos, sin):
    v = v * lax.rsqrt(jnp.mean(v * v, axis=0, keepdims=True) + norm_eps)
    swapped = jnp.concatenate([v[HD // 2 :], v[: HD // 2]], axis=0)
    return v * cos + swapped * sin


def places(rows):
    core = lax.rem(lax.axis_index("gy"), 2)
    for half in (core, 1 - core):
        yield pl.ds(pl.multiple_of(half * rows, rows), rows)


def project_kv_kernel(weight, q_weight, *refs):
    (left, before), (left_other, before_other), (cosine, sine, kv_out) = refs[0:2], refs[2:4], refs[4:]
    turned_weight = weight[...].T
    halves = ((left, before), (left_other, before_other))
    for (block, total), at in zip(halves, places(left.shape[1])):
        product = jnp.dot(turned_weight, block[...], preferred_element_type=jnp.float32)
        values = (total[0 : 2 * HD, :] + product).astype(jnp.bfloat16)
        key = turned(values[0:HD].astype(jnp.float32), cosine[:, at], sine[:, at])
        kv_out[0:HD, at] = key.astype(jnp.bfloat16)
        kv_out[HD : 2 * HD, at] = values[HD : 2 * HD]


def project_q_kernel(weight, kv, *refs):
    (left, before), (left_other, before_other), (cosine, sine, q_out) = refs[0:2], refs[2:4], refs[4:]
    turned_weight = weight[...].T
    halves = ((left, before), (left_other, before_other))
    for (block, total), at in zip(halves, places(left.shape[1])):
        product = jnp.dot(turned_weight, block[...], preferred_element_type=jnp.float32)
        values = (total[2 * HD : 4 * HD, :] + product).astype(jnp.bfloat16).astype(jnp.float32)
        for h in range(2):
            part = slice(h * HD, (h + 1) * HD)
            query = turned(values[part], cosine[:, at], sine[:, at]) * query_scale
            q_out[part, at] = query.astype(jnp.bfloat16)


LIGHT = pl.CostEstimate(flops=1024, bytes_accessed=1024, transcendentals=0)
ANY_SPEC = pl.BlockSpec(memory_space=pl.ANY)
VMEM_SPEC = pl.BlockSpec(memory_space=pltpu.VMEM)


def project_most(blocks, early, late):
    width, rows = blocks[0].shape
    columns = early.shape[1]
    return pl.pallas_call(
        project_most_kernel,
        out_shape=(
            jax.ShapeDtypeStruct((columns, rows), jnp.float32),
            jax.ShapeDtypeStruct((width, rows), jnp.bfloat16),
        ),
        in_specs=[VMEM_SPEC] * 10,
        out_specs=(VMEM_SPEC, VMEM_SPEC),
        compiler_params=pltpu.CompilerParams(vmem_limit_bytes=20 * MIB),
        cost_estimate=pl.CostEstimate(
            flops=14 * rows * width * columns, bytes_accessed=15 * MIB, transcendentals=0
        ),
        name="project_most",
    )(*blocks, early, late)


def project_rest(kernel, weight, after, most, most_other, cosine, sine):
    (total, left), (total_other, left_other) = most, most_other
    return pl.pallas_call(
        kernel,
        out_shape=jax.ShapeDtypeStruct((weight.shape[1], 2 * left.shape[1]), jnp.bfloat16),
        in_specs=[VMEM_SPEC, ANY_SPEC] + [VMEM_SPEC] * 6,
        out_specs=VMEM_SPEC,
        compiler_params=pltpu.CompilerParams(vmem_limit_bytes=16 * MIB),
        cost_estimate=LIGHT,
        name="project_rest",
    )(weight, after, left, total, left_other, total_other, cosine, sine)


def small_call(kernel, out_shape, *args, in_specs=None):
    return pl.pallas_call(
        kernel,
        out_shape=out_shape,
        in_specs=in_specs or [VMEM_SPEC] * len(args),
        out_specs=jax.tree.map(lambda _: VMEM_SPEC, out_shape),
        compiler_params=pltpu.CompilerParams(vmem_limit_bytes=8 * MIB),
        cost_estimate=LIGHT,
        name="small",
    )(*args)


def angles_kernel(start, frequency, cosine, sine):
    rows = cosine.shape[1]
    chip = lax.div(lax.axis_index("gy"), 2)
    column = lax.broadcasted_iota(jnp.int32, (HD // 2, rows), 1)
    positions = (start[0] + chip * rows + column).astype(jnp.float32)
    angles = positions * frequency[...]
    cos, sin = jnp.cos(angles), jnp.sin(angles)
    cosine[0 : HD // 2, :] = cos
    cosine[HD // 2 : HD, :] = cos
    sine[0 : HD // 2, :] = -sin
    sine[HD // 2 : HD, :] = sin


def angles_of(start, rows):
    frequency = 10000.0 ** (-2.0 * np.arange(HD // 2) / HD)
    frequency = jnp.asarray(np.repeat(frequency[:, None], rows, axis=1), jnp.float32)
    shape = jax.ShapeDtypeStruct((HD, rows), jnp.float32)
    specs = [pl.BlockSpec(memory_space=pltpu.SMEM), VMEM_SPEC]
    return small_call(angles_kernel, (shape, shape), start, frequency, in_specs=specs)


def beside_kernel(left, right, out):
    columns = left.shape[1]
    out[:, 0:columns] = left[...]
    out[:, columns : 2 * columns] = right[...]


def beside(left, right):
    rows, columns = left.shape
    shape = jax.ShapeDtypeStruct((rows, 2 * columns), left.dtype)
    return small_call(beside_kernel, shape, left, right)


def halves_kernel(first, second, low, high):
    columns = low.shape[1]
    low[...] = first[:, 0:columns]
    high[...] = second[:, columns : 2 * columns]


def halves(first, second):
    rows, columns = first.shape
    shape = jax.ShapeDtypeStruct((rows, columns // 2), first.dtype)
    return small_call(halves_kernel, (shape, shape), first, second)


QB = 256


def window(q_ref, kv_ref, keys, i, low):
    count = q_ref.shape[1] // QB
    first, last = (0, i + 1) if low else (i, count)
    at = pl.ds(i * QB, QB)
    query = jnp.concatenate([q_ref[0:HD, at], q_ref[HD : 2 * HD, at]], axis=1)
    total, weight = None, None
    for j in range(first, last):
        here = slice(j * QB, (j + 1) * QB)
        e = jnp.exp(jnp.dot(keys[here], query, preferred_element_type=jnp.float32))
        if j == i:
            key = lax.broadcasted_iota(jnp.int32, (QB, QB), 0)
            column = lax.broadcasted_iota(jnp.int32, (QB, QB), 1)
            keep = key <= column if low else key > column
            e = jnp.where(jnp.concatenate([keep, keep], axis=1), e, 0.0)
        w = jnp.sum(e, axis=0, keepdims=True)
        t = jnp.dot(
            kv_ref[HD : 2 * HD, here], e.astype(jnp.bfloat16), preferred_element_type=jnp.float32
        )
        total = t if total is None else total + t
        weight = w if weight is None else weight + w
    return total, weight


def own_kernel(q_ref, kv_ref, total_ref, weight_ref, keys):
    keys[...] = kv_ref[0:HD, :].T
    for i in range(q_ref.shape[1] // QB):
        total, weight = window(q_ref, kv_ref, keys, i, True)
        for h in range(2):
            part = slice(h * QB, (h + 1) * QB)
            at = pl.ds(i * QB, QB)
            total_ref[h * HD : (h + 1) * HD, at] = total[:, part]
            weight_ref[h : h + 1, at] = weight[:, part]


def before_kernel(q_ref, sent_ref, cached_ref, total_ref, weight_ref, mixed_ref, kv_ref, keys):
    chip = lax.div(lax.axis_index("gy"), 2)

    @pl.when(chip == 0)
    def _():
        kv_ref[...] = cached_ref[...]

    @pl.when(chip > 0)
    def _():
        kv_ref[...] = sent_ref[...]

    keys[...] = kv_ref[0:HD, :].T
    for i in range(q_ref.shape[1] // QB):
        total, weight = window(q_ref, kv_ref, keys, i, False)
        for h in range(2):
            part = slice(h * QB, (h + 1) * QB)
            at = pl.ds(i * QB, QB)
            row = slice(h * HD, (h + 1) * HD)
            top = total[:, part] + total_ref[row, at]
            low = weight[:, part] + weight_ref[h : h + 1, at]
            mixed_ref[row, at] = (top / low).astype(jnp.bfloat16)


def attend_own(q, kv):
    rows = q.shape[1]
    return pl.pallas_call(
        own_kernel,
        out_shape=(
            jax.ShapeDtypeStruct(q.shape, jnp.float32),
            jax.ShapeDtypeStruct((2, rows), jnp.float32),
        ),
        scratch_shapes=[pltpu.VMEM((rows, HD), jnp.bfloat16)],
        compiler_params=pltpu.CompilerParams(vmem_limit_bytes=20 * MIB),
        cost_estimate=LIGHT,
        name="attend_own",
    )(q, kv)


def attend_before(q, sent, cached, total, weight):
    rows = q.shape[1]
    return pl.pallas_call(
        before_kernel,
        out_shape=jax.ShapeDtypeStruct(q.shape, jnp.bfloat16),
        scratch_shapes=[
            pltpu.VMEM(sent.shape, jnp.bfloat16),
            pltpu.VMEM((rows, HD), jnp.bfloat16),
        ],
        compiler_params=pltpu.CompilerParams(vmem_limit_bytes=20 * MIB),
        cost_estimate=LIGHT,
        name="attend_before",
    )(q, sent, cached, total, weight)


def out_most_kernel(*refs):
    mixed, weights = refs[0:7], refs[7:15]
    total, left, held_m, held_w, sems = refs[15:]
    depth = mixed[0].shape[0]
    slots = out_slots()
    copies = []
    for i in range(8):
        to = held_w.at[:, pl.ds(pl.multiple_of(slots[i] * depth, depth), depth)]
        copies.append(pltpu.make_async_copy(weights[i], to, sems.at[8 + i]))
    for i in range(7):
        here = held_m.at[pl.ds(i * depth, depth), :]
        copies.append(pltpu.make_async_copy(mixed[i], here, sems.at[i]))
    for copy in copies:
        copy.start()
    for copy in copies:
        copy.wait()
    rows = total.shape[2]
    left[...] = held_w[:, 7 * depth : 8 * depth]
    for half in range(2):
        here = held_m[:, half * rows : (half + 1) * rows]
        total[half] = jnp.dot(
            held_w[:, 0 : 7 * depth], here, preferred_element_type=jnp.float32
        )


def out_rest_kernel(flip, left, low, high, total, out):
    core = lax.rem(lax.axis_index("gy"), 2)
    half = 1 - core if flip else core
    for side, mixed in enumerate((low, high)):

        @pl.when(half == side)
        def _():
            product = jnp.dot(left[...], mixed[...], preferred_element_type=jnp.float32)
            out[...] = (total[side] + product).astype(out.dtype)


def out_most(mixed, weights):
    width, depth = weights[0].shape
    rows = mixed[0].shape[1] // 2
    return pl.pallas_call(
        out_most_kernel,
        out_shape=(
            jax.ShapeDtypeStruct((2, width, rows), jnp.float32),
            jax.ShapeDtypeStruct((width, depth), jnp.bfloat16),
        ),
        in_specs=[ANY_SPEC] * 15,
        out_specs=(VMEM_SPEC, VMEM_SPEC),
        scratch_shapes=[
            pltpu.VMEM((7 * depth, 2 * rows), jnp.bfloat16),
            pltpu.VMEM((width, 8 * depth), jnp.bfloat16),
            pltpu.SemaphoreType.DMA((16,)),
        ],
        compiler_params=pltpu.CompilerParams(vmem_limit_bytes=20 * MIB),
        cost_estimate=LIGHT,
        name="out_most",
    )(*mixed, *weights)


def out_rest(left, low, high, total, kind, flip):
    return pl.pallas_call(
        functools.partial(out_rest_kernel, flip),
        out_shape=jax.ShapeDtypeStruct(total.shape[1:], kind),
        in_specs=[VMEM_SPEC] * 4,
        out_specs=VMEM_SPEC,
        compiler_params=pltpu.CompilerParams(vmem_limit_bytes=20 * MIB),
        cost_estimate=LIGHT,
        name="out_rest",
    )(left, low, high, total)


def shards(hidden, start, w_query, w_key_value, w_out, cache):
    rows, width = hidden.shape
    kv_weight = w_key_value.reshape(width, 2 * HD)
    kv_weight, hidden = together(kv_weight, hidden)
    block = hidden.T
    out_block = w_out.T

    moved_q, moved_kv = shear_y(w_query), shear_y(kv_weight)
    block_z = swap_zh(block)
    block_r, block_l = shift_x(block, 1), shift_x(block, -1)
    moved_q, moved_kv, block_z, block_r, block_l, out_block, cache = together(
        moved_q, moved_kv, block_z, block_r, block_l, out_block, cache
    )
    moved = turn_x(beside(moved_kv, moved_q))
    out_r, out_l = shift_y(out_block, 1), shift_y(out_block, -1)
    other = [swap_core(block), swap_core(block_z), swap_core(block_r)]
    cosine, sine = angles_of(start, 2 * rows)
    moved, block_z, block_r, block_l, out_r, out_l, cosine, sine, *other = together(
        moved, block_z, block_r, block_l, out_r, out_l, cosine, sine, *other
    )
    moved_z = swap_zl(moved)
    moved_r, moved_l = shift_y(moved, 1), shift_y(moved, -1)
    block_zr, block_zl = shift_x(block_z, 1), shift_x(block_z, -1)
    moved_z, moved_r, moved_l, block_zr, block_zl, block_r, block_l = together(
        moved_z, moved_r, moved_l, block_zr, block_zl, block_r, block_l
    )
    moved_f, moved_zl, moved_zr = shift_y(moved_r, 1), shift_y(moved_z, -1), swap_zl(moved_r)
    block_f, block_zf = shift_x(block_r, 1), shift_x(block_zl, -1)
    early = turn([moved, moved_z, moved_r, moved_l])
    moved_f, moved_zr, moved_zl, block_f, block_zf, cache, early = together(
        moved_f, moved_zr, moved_zl, block_f, block_zf, cache, early
    )
    half_zl, half_zr = halves(moved_zl, moved_zr)
    last_kv, last_q = shift_y(half_zl, -1), shift_y(half_zr, 1)
    late = turn([moved_zr, moved_zl, moved_f])
    own = [block, block_z, block_r, block_l, block_zr, block_zl, block_f, block_zf]
    other += [swap_core(b) for b in (block_l, block_zr, block_zl, block_f, block_zf)]
    pairs = []
    for gx in range(8):
        head = 8 * (gx % 2) + 2 * (gx // 2)
        pairs += [(gx * 16 + head + c, gx * 16 + c) for c in range(2)]
    cached = lax.ppermute(cache, AXES, pairs)
    most = project_most(own, early, late)
    most_other = project_most(other, early, late)
    kv = project_rest(project_kv_kernel, last_kv, last_q, most, most_other, cosine, sine)
    before = lax.ppermute(kv, "gy", [(i, i + 2) for i in range(14)])
    q = project_rest(project_q_kernel, last_q, kv, most, most_other, cosine, sine)

    kv, q, out_block, out_r, out_l, cached = together(kv, q, out_block, out_r, out_l, cached)
    cached = cached.reshape(2 * rows, 2 * HD).T
    out_z, out_f = swap_zl(out_block), shift_y(out_l, -1)
    total, weight_sum = attend_own(q, kv)
    mixed = attend_before(q, before, cached, total, weight_sum)

    mixed_z = swap_zh(mixed)
    mixed_r, mixed_l = shift_x(mixed, 1), shift_x(mixed, -1)
    out_zr, out_zl = shift_y(out_z, 1), shift_y(out_z, -1)
    mixed_z, mixed_r, mixed_l, out_zr, out_zl = together(mixed_z, mixed_r, mixed_l, out_zr, out_zl)
    mixed_f, mixed_zl, mixed_zr = shift_x(mixed_r, 1), shift_x(mixed_z, -1), swap_zh(mixed_r)
    out_zf = shift_y(out_zl, -1)
    mixed_f, mixed_zr, mixed_zl, out_zf = together(mixed_f, mixed_zr, mixed_zl, out_zf)
    low, high = halves(mixed_zr, mixed_zl)
    low, high = shift_x(low, 1), shift_x(high, -1)
    outs = [out_block, out_z, out_r, out_l, out_zr, out_zl, out_f, out_zf]
    gathered = [mixed, mixed_z, mixed_r, mixed_l, mixed_zr, mixed_zl, mixed_f]
    total, left = out_most(gathered, outs)
    sent = swap_core(out_rest(left, low, high, total, jnp.bfloat16, True))
    kept = out_rest(left, low, high, total, jnp.float32, False)
    return (kept + sent.astype(jnp.float32)).astype(jnp.bfloat16).T


def solution(mesh):
    return jax.shard_map(
        shards,
        mesh=mesh,
        in_specs=(
            P("gy", "gx"),
            P(),
            P("gx", "gy"),
            P("gx", None, "gy"),
            P("gy", "gx"),
            P(None, None, "gy"),
        ),
        out_specs=P("gy", "gx"),
        check_vma=False,
    )
```

```python
import functools

import jax
import jax.numpy as jnp
import numpy as np
from jax import lax
from jax.experimental import pallas as pl
from jax.experimental.pallas import tpu as pltpu
from jax.sharding import PartitionSpec as P

HD = 128
AXES = ("gx", "gy")
MIB = 1024 * 1024

query_scale = 168.0 ** (-0.5)
norm_eps = 1e-06


def place(index):
    gx, gy = divmod(index, 16)
    x, zh = divmod(gx, 2)
    zl, rest = divmod(gy, 8)
    y, core = divmod(rest, 2)
    return x, zh, zl, y, core


def number(x, zh, zl, y, core):
    return ((x % 4) * 2 + zh) * 16 + zl * 8 + (y % 4) * 2 + core


def move(value, to):
    return lax.ppermute(value, AXES, [(i, number(*to(*place(i)))) for i in range(128)])


def shift_x(value, by):
    return move(value, lambda x, zh, zl, y, c: (x + by, zh, zl, y, c))


def shift_y(value, by):
    return move(value, lambda x, zh, zl, y, c: (x, zh, zl, y + by, c))


def swap_zh(value):
    return move(value, lambda x, zh, zl, y, c: (x, 1 - zh, zl, y, c))


def swap_zl(value):
    return move(value, lambda x, zh, zl, y, c: (x, zh, 1 - zl, y, c))


def swap_core(value):
    return move(value, lambda x, zh, zl, y, c: (x, zh, zl, y, 1 - c))


def shear_y(value):
    return move(value, lambda x, zh, zl, y, c: (x, zh, zl, y + x, c))


def turn_x(value):
    return move(value, lambda x, zh, zl, y, c: (y - x, zl, zh, y, c))


def together(*values):
    return lax.optimization_barrier(values)


OFFSETS = ((0, 0), (0, 1), (3, 0), (1, 0), (3, 1), (1, 1), (2, 0), (2, 1))


def index_of(ring, pair):
    ring, pair = lax.rem(ring + 8, 4), lax.rem(pair, 2)
    base = jnp.where(ring == 0, 0, jnp.where(ring == 3, 2, jnp.where(ring == 1, 3, 6)))
    step = jnp.where((ring == 0) | (ring == 2), 1, 2)
    return base + step * pair


def coordinates():
    gx, gy = lax.axis_index("gx"), lax.axis_index("gy")
    zl, rest = lax.div(gy, 8), lax.rem(gy, 8)
    return lax.div(gx, 2), lax.rem(gx, 2), zl, lax.div(rest, 2), lax.rem(rest, 2)


def out_slots():
    x, zh, zl, y, core = coordinates()
    return [index_of(y + d - x, zl + e + zh) for d, e in OFFSETS]


def hidden_slots():
    x, zh, zl, y, core = coordinates()
    return [index_of(2 * x + d - y, zh + e + zl) for d, e in OFFSETS]


def turn_kernel(*refs):
    blocks, out = refs[:-1], refs[-1]
    for i, block in enumerate(blocks):
        out[i] = block[...].T


def turn(blocks):
    width, columns = blocks[0].shape
    shape = jax.ShapeDtypeStruct((len(blocks), columns, width), blocks[0].dtype)
    return small_call(turn_kernel, shape, *blocks)


def project_most_kernel(*refs):
    blocks, early, late, total, left = refs[0:8], refs[8], refs[9], refs[10], refs[11]
    slots = hidden_slots()
    total[...] = jnp.zeros_like(total)
    for j in range(8):

        @pl.when(slots[j] < 4)
        def _():
            weight = early[jnp.minimum(slots[j], 3)]
            total[...] += jnp.dot(weight, blocks[j][...], preferred_element_type=jnp.float32)

        @pl.when((slots[j] >= 4) & (slots[j] < 7))
        def _():
            weight = late[jnp.clip(slots[j] - 4, 0, 2)]
            total[...] += jnp.dot(weight, blocks[j][...], preferred_element_type=jnp.float32)

        @pl.when(slots[j] == 7)
        def _():
            left[...] = blocks[j][...]


def turned(v, cos, sin):
    v = v * lax.rsqrt(jnp.mean(v * v, axis=0, keepdims=True) + norm_eps)
    swapped = jnp.concatenate([v[HD // 2 :], v[: HD // 2]], axis=0)
    return v * cos + swapped * sin


def places(rows):
    core = lax.rem(lax.axis_index("gy"), 2)
    for half in (core, 1 - core):
        yield pl.ds(pl.multiple_of(half * rows, rows), rows)


def project_kv_kernel(weight, q_weight, *refs):
    (left, before), (left_other, before_other), (cosine, sine, kv_out) = refs[0:2], refs[2:4], refs[4:]
    turned_weight = weight[...].T
    halves = ((left, before), (left_other, before_other))
    for (block, total), at in zip(halves, places(left.shape[1])):
        product = jnp.dot(turned_weight, block[...], preferred_element_type=jnp.float32)
        values = (total[0 : 2 * HD, :] + product).astype(jnp.bfloat16)
        key = turned(values[0:HD].astype(jnp.float32), cosine[:, at], sine[:, at])
        kv_out[0:HD, at] = key.astype(jnp.bfloat16)
        kv_out[HD : 2 * HD, at] = values[HD : 2 * HD]


def project_q_kernel(weight, kv, *refs):
    (left, before), (left_other, before_other), (cosine, sine, q_out) = refs[0:2], refs[2:4], refs[4:]
    turned_weight = weight[...].T
    halves = ((left, before), (left_other, before_other))
    for (block, total), at in zip(halves, places(left.shape[1])):
        product = jnp.dot(turned_weight, block[...], preferred_element_type=jnp.float32)
        values = (total[2 * HD : 4 * HD, :] + product).astype(jnp.bfloat16).astype(jnp.float32)
        for h in range(2):
            part = slice(h * HD, (h + 1) * HD)
            query = turned(values[part], cosine[:, at], sine[:, at]) * query_scale
            q_out[part, at] = query.astype(jnp.bfloat16)


LIGHT = pl.CostEstimate(flops=1024, bytes_accessed=1024, transcendentals=0)
ANY_SPEC = pl.BlockSpec(memory_space=pl.ANY)
VMEM_SPEC = pl.BlockSpec(memory_space=pltpu.VMEM)


def project_most(blocks, early, late):
    width, rows = blocks[0].shape
    columns = early.shape[1]
    return pl.pallas_call(
        project_most_kernel,
        out_shape=(
            jax.ShapeDtypeStruct((columns, rows), jnp.float32),
            jax.ShapeDtypeStruct((width, rows), jnp.bfloat16),
        ),
        in_specs=[VMEM_SPEC] * 10,
        out_specs=(VMEM_SPEC, VMEM_SPEC),
        compiler_params=pltpu.CompilerParams(vmem_limit_bytes=20 * MIB),
        cost_estimate=pl.CostEstimate(
            flops=14 * rows * width * columns, bytes_accessed=15 * MIB, transcendentals=0
        ),
        name="project_most",
    )(*blocks, early, late)


def project_rest(kernel, weight, after, most, most_other, cosine, sine):
    (total, left), (total_other, left_other) = most, most_other
    return pl.pallas_call(
        kernel,
        out_shape=jax.ShapeDtypeStruct((weight.shape[1], 2 * left.shape[1]), jnp.bfloat16),
        in_specs=[VMEM_SPEC, ANY_SPEC] + [VMEM_SPEC] * 6,
        out_specs=VMEM_SPEC,
        compiler_params=pltpu.CompilerParams(vmem_limit_bytes=16 * MIB),
        cost_estimate=LIGHT,
        name="project_rest",
    )(weight, after, left, total, left_other, total_other, cosine, sine)


def small_call(kernel, out_shape, *args, in_specs=None):
    return pl.pallas_call(
        kernel,
        out_shape=out_shape,
        in_specs=in_specs or [VMEM_SPEC] * len(args),
        out_specs=jax.tree.map(lambda _: VMEM_SPEC, out_shape),
        compiler_params=pltpu.CompilerParams(vmem_limit_bytes=8 * MIB),
        cost_estimate=LIGHT,
        name="small",
    )(*args)


def angles_kernel(start, frequency, cosine, sine):
    rows = cosine.shape[1]
    chip = lax.div(lax.axis_index("gy"), 2)
    column = lax.broadcasted_iota(jnp.int32, (HD // 2, rows), 1)
    positions = (start[0] + chip * rows + column).astype(jnp.float32)
    angles = positions * frequency[...]
    cos, sin = jnp.cos(angles), jnp.sin(angles)
    cosine[0 : HD // 2, :] = cos
    cosine[HD // 2 : HD, :] = cos
    sine[0 : HD // 2, :] = -sin
    sine[HD // 2 : HD, :] = sin


def angles_of(start, rows):
    frequency = 10000.0 ** (-2.0 * np.arange(HD // 2) / HD)
    frequency = jnp.asarray(np.repeat(frequency[:, None], rows, axis=1), jnp.float32)
    shape = jax.ShapeDtypeStruct((HD, rows), jnp.float32)
    specs = [pl.BlockSpec(memory_space=pltpu.SMEM), VMEM_SPEC]
    return small_call(angles_kernel, (shape, shape), start, frequency, in_specs=specs)


def beside_kernel(left, right, out):
    columns = left.shape[1]
    out[:, 0:columns] = left[...]
    out[:, columns : 2 * columns] = right[...]


def beside(left, right):
    rows, columns = left.shape
    shape = jax.ShapeDtypeStruct((rows, 2 * columns), left.dtype)
    return small_call(beside_kernel, shape, left, right)


def halves_kernel(first, second, low, high):
    columns = low.shape[1]
    low[...] = first[:, 0:columns]
    high[...] = second[:, columns : 2 * columns]


def halves(first, second):
    rows, columns = first.shape
    shape = jax.ShapeDtypeStruct((rows, columns // 2), first.dtype)
    return small_call(halves_kernel, (shape, shape), first, second)


QB = 256


def window(q_ref, kv_ref, keys, i, low):
    count = q_ref.shape[1] // QB
    first, last = (0, i + 1) if low else (i, count)
    at = pl.ds(i * QB, QB)
    query = jnp.concatenate([q_ref[0:HD, at], q_ref[HD : 2 * HD, at]], axis=1)
    total, weight = None, None
    for j in range(first, last):
        here = slice(j * QB, (j + 1) * QB)
        e = jnp.exp(jnp.dot(keys[here], query, preferred_element_type=jnp.float32))
        if j == i:
            key = lax.broadcasted_iota(jnp.int32, (QB, QB), 0)
            column = lax.broadcasted_iota(jnp.int32, (QB, QB), 1)
            keep = key <= column if low else key > column
            e = jnp.where(jnp.concatenate([keep, keep], axis=1), e, 0.0)
        w = jnp.sum(e, axis=0, keepdims=True)
        t = jnp.dot(
            kv_ref[HD : 2 * HD, here], e.astype(jnp.bfloat16), preferred_element_type=jnp.float32
        )
        total = t if total is None else total + t
        weight = w if weight is None else weight + w
    return total, weight


def own_kernel(q_ref, kv_ref, total_ref, weight_ref, keys):
    keys[...] = kv_ref[0:HD, :].T
    for i in range(q_ref.shape[1] // QB):
        total, weight = window(q_ref, kv_ref, keys, i, True)
        for h in range(2):
            part = slice(h * QB, (h + 1) * QB)
            at = pl.ds(i * QB, QB)
            total_ref[h * HD : (h + 1) * HD, at] = total[:, part]
            weight_ref[h : h + 1, at] = weight[:, part]


def before_kernel(q_ref, sent_ref, cached_ref, total_ref, weight_ref, mixed_ref, kv_ref, keys):
    chip = lax.div(lax.axis_index("gy"), 2)

    @pl.when(chip == 0)
    def _():
        kv_ref[...] = cached_ref[...]

    @pl.when(chip > 0)
    def _():
        kv_ref[...] = sent_ref[...]

    keys[...] = kv_ref[0:HD, :].T
    for i in range(q_ref.shape[1] // QB):
        total, weight = window(q_ref, kv_ref, keys, i, False)
        for h in range(2):
            part = slice(h * QB, (h + 1) * QB)
            at = pl.ds(i * QB, QB)
            row = slice(h * HD, (h + 1) * HD)
            top = total[:, part] + total_ref[row, at]
            low = weight[:, part] + weight_ref[h : h + 1, at]
            mixed_ref[row, at] = (top / low).astype(jnp.bfloat16)


def attend_own(q, kv):
    rows = q.shape[1]
    return pl.pallas_call(
        own_kernel,
        out_shape=(
            jax.ShapeDtypeStruct(q.shape, jnp.float32),
            jax.ShapeDtypeStruct((2, rows), jnp.float32),
        ),
        scratch_shapes=[pltpu.VMEM((rows, HD), jnp.bfloat16)],
        compiler_params=pltpu.CompilerParams(vmem_limit_bytes=20 * MIB),
        cost_estimate=LIGHT,
        name="attend_own",
    )(q, kv)


def attend_before(q, sent, cached, total, weight):
    rows = q.shape[1]
    return pl.pallas_call(
        before_kernel,
        out_shape=jax.ShapeDtypeStruct(q.shape, jnp.bfloat16),
        scratch_shapes=[
            pltpu.VMEM(sent.shape, jnp.bfloat16),
            pltpu.VMEM((rows, HD), jnp.bfloat16),
        ],
        compiler_params=pltpu.CompilerParams(vmem_limit_bytes=20 * MIB),
        cost_estimate=LIGHT,
        name="attend_before",
    )(q, sent, cached, total, weight)


def out_most_kernel(*refs):
    mixed, weights = refs[0:7], refs[7:15]
    total, left, held_m, held_w, sems = refs[15:]
    depth = mixed[0].shape[0]
    slots = out_slots()
    copies = []
    for i in range(8):
        to = held_w.at[:, pl.ds(pl.multiple_of(slots[i] * depth, depth), depth)]
        copies.append(pltpu.make_async_copy(weights[i], to, sems.at[8 + i]))
    for i in range(7):
        here = held_m.at[pl.ds(i * depth, depth), :]
        copies.append(pltpu.make_async_copy(mixed[i], here, sems.at[i]))
    for copy in copies:
        copy.start()
    for copy in copies:
        copy.wait()
    rows = total.shape[2]
    left[...] = held_w[:, 7 * depth : 8 * depth]
    for half in range(2):
        here = held_m[:, half * rows : (half + 1) * rows]
        total[half] = jnp.dot(
            held_w[:, 0 : 7 * depth], here, preferred_element_type=jnp.float32
        )


def out_rest_kernel(flip, left, low, high, total, out):
    core = lax.rem(lax.axis_index("gy"), 2)
    half = 1 - core if flip else core
    for side, mixed in enumerate((low, high)):

        @pl.when(half == side)
        def _():
            product = jnp.dot(left[...], mixed[...], preferred_element_type=jnp.float32)
            out[...] = (total[side] + product).astype(out.dtype)


def out_most(mixed, weights):
    width, depth = weights[0].shape
    rows = mixed[0].shape[1] // 2
    return pl.pallas_call(
        out_most_kernel,
        out_shape=(
            jax.ShapeDtypeStruct((2, width, rows), jnp.float32),
            jax.ShapeDtypeStruct((width, depth), jnp.bfloat16),
        ),
        in_specs=[ANY_SPEC] * 15,
        out_specs=(VMEM_SPEC, VMEM_SPEC),
        scratch_shapes=[
            pltpu.VMEM((7 * depth, 2 * rows), jnp.bfloat16),
            pltpu.VMEM((width, 8 * depth), jnp.bfloat16),
            pltpu.SemaphoreType.DMA((16,)),
        ],
        compiler_params=pltpu.CompilerParams(vmem_limit_bytes=20 * MIB),
        cost_estimate=LIGHT,
        name="out_most",
    )(*mixed, *weights)


def out_rest(left, low, high, total, kind, flip):
    return pl.pallas_call(
        functools.partial(out_rest_kernel, flip),
        out_shape=jax.ShapeDtypeStruct(total.shape[1:], kind),
        in_specs=[VMEM_SPEC] * 4,
        out_specs=VMEM_SPEC,
        compiler_params=pltpu.CompilerParams(vmem_limit_bytes=20 * MIB),
        cost_estimate=LIGHT,
        name="out_rest",
    )(left, low, high, total)


def shards(hidden, start, w_query, w_key_value, w_out, cache):
    rows, width = hidden.shape
    kv_weight = w_key_value.reshape(width, 2 * HD)
    kv_weight, hidden = together(kv_weight, hidden)
    block = hidden.T
    out_block = w_out.T

    moved_q, moved_kv = shear_y(w_query), shear_y(kv_weight)
    block_z = swap_zh(block)
    block_r, block_l = shift_x(block, 1), shift_x(block, -1)
    moved_q, moved_kv, block_z, block_r, block_l, out_block, cache = together(
        moved_q, moved_kv, block_z, block_r, block_l, out_block, cache
    )
    moved = turn_x(beside(moved_kv, moved_q))
    out_r, out_l = shift_y(out_block, 1), shift_y(out_block, -1)
    other = [swap_core(block), swap_core(block_z), swap_core(block_r)]
    cosine, sine = angles_of(start, 2 * rows)
    moved, block_z, block_r, block_l, out_r, out_l, cosine, sine, *other = together(
        moved, block_z, block_r, block_l, out_r, out_l, cosine, sine, *other
    )
    moved_z = swap_zl(moved)
    moved_r, moved_l = shift_y(moved, 1), shift_y(moved, -1)
    block_zr, block_zl = shift_x(block_z, 1), shift_x(block_z, -1)
    moved_z, moved_r, moved_l, block_zr, block_zl, block_r, block_l = together(
        moved_z, moved_r, moved_l, block_zr, block_zl, block_r, block_l
    )
    moved_f, moved_zl, moved_zr = shift_y(moved_r, 1), shift_y(moved_z, -1), swap_zl(moved_r)
    block_f, block_zf = shift_x(block_r, 1), shift_x(block_zl, -1)
    early = turn([moved, moved_z, moved_r, moved_l])
    moved_f, moved_zr, moved_zl, block_f, block_zf, cache, early = together(
        moved_f, moved_zr, moved_zl, block_f, block_zf, cache, early
    )
    half_zl, half_zr = halves(moved_zl, moved_zr)
    last_kv, last_q = shift_y(half_zl, -1), shift_y(half_zr, 1)
    late = turn([moved_zr, moved_zl, moved_f])
    own = [block, block_z, block_r, block_l, block_zr, block_zl, block_f, block_zf]
    other += [swap_core(b) for b in (block_l, block_zr, block_zl, block_f, block_zf)]
    pairs = []
    for gx in range(8):
        head = 8 * (gx % 2) + 2 * (gx // 2)
        pairs += [(gx * 16 + head + c, gx * 16 + c) for c in range(2)]
    cached = lax.ppermute(cache, AXES, pairs)
    most = project_most(own, early, late)
    most_other = project_most(other, early, late)
    kv = project_rest(project_kv_kernel, last_kv, last_q, most, most_other, cosine, sine)
    before = lax.ppermute(kv, "gy", [(i, i + 2) for i in range(14)])
    q = project_rest(project_q_kernel, last_q, kv, most, most_other, cosine, sine)

    kv, q, out_block, out_r, out_l = together(kv, q, out_block, out_r, out_l)
    out_z, out_f = swap_zl(out_block), shift_y(out_l, -1)
    total, weight_sum = attend_own(q, kv)
    total, weight_sum, cached = together(total, weight_sum, cached)
    cached = cached.reshape(2 * rows, 2 * HD).T
    mixed = attend_before(q, before, cached, total, weight_sum)

    mixed_z = swap_zh(mixed)
    mixed_r, mixed_l = shift_x(mixed, 1), shift_x(mixed, -1)
    out_zr, out_zl = shift_y(out_z, 1), shift_y(out_z, -1)
    mixed_z, mixed_r, mixed_l, out_zr, out_zl = together(mixed_z, mixed_r, mixed_l, out_zr, out_zl)
    mixed_f, mixed_zl, mixed_zr = shift_x(mixed_r, 1), shift_x(mixed_z, -1), swap_zh(mixed_r)
    out_zf = shift_y(out_zl, -1)
    mixed_f, mixed_zr, mixed_zl, out_zf = together(mixed_f, mixed_zr, mixed_zl, out_zf)
    low, high = halves(mixed_zr, mixed_zl)
    low, high = shift_x(low, 1), shift_x(high, -1)
    outs = [out_block, out_z, out_r, out_l, out_zr, out_zl, out_f, out_zf]
    gathered = [mixed, mixed_z, mixed_r, mixed_l, mixed_zr, mixed_zl, mixed_f]
    total, left = out_most(gathered, outs)
    sent = swap_core(out_rest(left, low, high, total, jnp.bfloat16, True))
    kept = out_rest(left, low, high, total, jnp.float32, False)
    return (kept + sent.astype(jnp.float32)).astype(jnp.bfloat16).T


def solution(mesh):
    return jax.shard_map(
        shards,
        mesh=mesh,
        in_specs=(
            P("gy", "gx"),
            P(),
            P("gx", "gy"),
            P("gx", None, "gy"),
            P("gy", "gx"),
            P(None, None, "gy"),
        ),
        out_specs=P("gy", "gx"),
        check_vma=False,
    )
```

```python
import functools

import jax
import jax.numpy as jnp
import numpy as np
from jax import lax
from jax.experimental import pallas as pl
from jax.experimental.pallas import tpu as pltpu
from jax.sharding import PartitionSpec as P

HD = 128
AXES = ("gx", "gy")
MIB = 1024 * 1024

query_scale = 168.0 ** (-0.5)
norm_eps = 1e-06


def place(index):
    gx, gy = divmod(index, 16)
    x, zh = divmod(gx, 2)
    zl, rest = divmod(gy, 8)
    y, core = divmod(rest, 2)
    return x, zh, zl, y, core


def number(x, zh, zl, y, core):
    return ((x % 4) * 2 + zh) * 16 + zl * 8 + (y % 4) * 2 + core


def move(value, to):
    return lax.ppermute(value, AXES, [(i, number(*to(*place(i)))) for i in range(128)])


def shift_x(value, by):
    return move(value, lambda x, zh, zl, y, c: (x + by, zh, zl, y, c))


def shift_y(value, by):
    return move(value, lambda x, zh, zl, y, c: (x, zh, zl, y + by, c))


def swap_zh(value):
    return move(value, lambda x, zh, zl, y, c: (x, 1 - zh, zl, y, c))


def swap_zl(value):
    return move(value, lambda x, zh, zl, y, c: (x, zh, 1 - zl, y, c))


def swap_core(value):
    return move(value, lambda x, zh, zl, y, c: (x, zh, zl, y, 1 - c))


def shear_y(value):
    return move(value, lambda x, zh, zl, y, c: (x, zh, zl, y + x, c))


def turn_x(value):
    return move(value, lambda x, zh, zl, y, c: (y - x, zl, zh, y, c))


def together(*values):
    return lax.optimization_barrier(values)


OFFSETS = ((0, 0), (0, 1), (3, 0), (1, 0), (3, 1), (1, 1), (2, 0), (2, 1))


def index_of(ring, pair):
    ring, pair = lax.rem(ring + 8, 4), lax.rem(pair, 2)
    base = jnp.where(ring == 0, 0, jnp.where(ring == 3, 2, jnp.where(ring == 1, 3, 6)))
    step = jnp.where((ring == 0) | (ring == 2), 1, 2)
    return base + step * pair


def coordinates():
    gx, gy = lax.axis_index("gx"), lax.axis_index("gy")
    zl, rest = lax.div(gy, 8), lax.rem(gy, 8)
    return lax.div(gx, 2), lax.rem(gx, 2), zl, lax.div(rest, 2), lax.rem(rest, 2)


def out_slots():
    x, zh, zl, y, core = coordinates()
    return [index_of(y + d - x, zl + e + zh) for d, e in OFFSETS]


def hidden_slots():
    x, zh, zl, y, core = coordinates()
    return [index_of(2 * x + d - y, zh + e + zl) for d, e in OFFSETS]


def turn_kernel(*refs):
    blocks, out = refs[:-1], refs[-1]
    for i, block in enumerate(blocks):
        out[i] = block[...].T


def turn(blocks):
    width, columns = blocks[0].shape
    shape = jax.ShapeDtypeStruct((len(blocks), columns, width), blocks[0].dtype)
    return small_call(turn_kernel, shape, *blocks)


def project_most_kernel(*refs):
    blocks, early, late, total, left = refs[0:8], refs[8], refs[9], refs[10], refs[11]
    slots = hidden_slots()
    total[...] = jnp.zeros_like(total)
    for j in range(8):

        @pl.when(slots[j] < 4)
        def _():
            weight = early[jnp.minimum(slots[j], 3)]
            total[...] += jnp.dot(weight, blocks[j][...], preferred_element_type=jnp.float32)

        @pl.when((slots[j] >= 4) & (slots[j] < 7))
        def _():
            weight = late[jnp.clip(slots[j] - 4, 0, 2)]
            total[...] += jnp.dot(weight, blocks[j][...], preferred_element_type=jnp.float32)

        @pl.when(slots[j] == 7)
        def _():
            left[...] = blocks[j][...]


def turned(v, cos, sin):
    v = v * lax.rsqrt(jnp.mean(v * v, axis=0, keepdims=True) + norm_eps)
    swapped = jnp.concatenate([v[HD // 2 :], v[: HD // 2]], axis=0)
    return v * cos + swapped * sin


def places(rows):
    core = lax.rem(lax.axis_index("gy"), 2)
    for half in (core, 1 - core):
        yield pl.ds(pl.multiple_of(half * rows, rows), rows)


def project_kv_kernel(weight, q_weight, *refs):
    (left, before), (left_other, before_other), (cosine, sine, kv_out) = refs[0:2], refs[2:4], refs[4:]
    turned_weight = weight[...].T
    halves = ((left, before), (left_other, before_other))
    for (block, total), at in zip(halves, places(left.shape[1])):
        product = jnp.dot(turned_weight, block[...], preferred_element_type=jnp.float32)
        values = (total[0 : 2 * HD, :] + product).astype(jnp.bfloat16)
        key = turned(values[0:HD].astype(jnp.float32), cosine[:, at], sine[:, at])
        kv_out[0:HD, at] = key.astype(jnp.bfloat16)
        kv_out[HD : 2 * HD, at] = values[HD : 2 * HD]


def project_q_kernel(weight, kv, *refs):
    (left, before), (left_other, before_other), (cosine, sine, q_out) = refs[0:2], refs[2:4], refs[4:]
    turned_weight = weight[...].T
    halves = ((left, before), (left_other, before_other))
    for (block, total), at in zip(halves, places(left.shape[1])):
        product = jnp.dot(turned_weight, block[...], preferred_element_type=jnp.float32)
        values = (total[2 * HD : 4 * HD, :] + product).astype(jnp.bfloat16).astype(jnp.float32)
        for h in range(2):
            part = slice(h * HD, (h + 1) * HD)
            query = turned(values[part], cosine[:, at], sine[:, at]) * query_scale
            q_out[part, at] = query.astype(jnp.bfloat16)


LIGHT = pl.CostEstimate(flops=1024, bytes_accessed=1024, transcendentals=0)
ANY_SPEC = pl.BlockSpec(memory_space=pl.ANY)
VMEM_SPEC = pl.BlockSpec(memory_space=pltpu.VMEM)


def project_most(blocks, early, late):
    width, rows = blocks[0].shape
    columns = early.shape[1]
    return pl.pallas_call(
        project_most_kernel,
        out_shape=(
            jax.ShapeDtypeStruct((columns, rows), jnp.float32),
            jax.ShapeDtypeStruct((width, rows), jnp.bfloat16),
        ),
        in_specs=[VMEM_SPEC] * 10,
        out_specs=(VMEM_SPEC, VMEM_SPEC),
        compiler_params=pltpu.CompilerParams(vmem_limit_bytes=20 * MIB),
        cost_estimate=pl.CostEstimate(
            flops=14 * rows * width * columns, bytes_accessed=15 * MIB, transcendentals=0
        ),
        name="project_most",
    )(*blocks, early, late)


def project_rest(kernel, weight, after, most, most_other, cosine, sine):
    (total, left), (total_other, left_other) = most, most_other
    return pl.pallas_call(
        kernel,
        out_shape=jax.ShapeDtypeStruct((weight.shape[1], 2 * left.shape[1]), jnp.bfloat16),
        in_specs=[VMEM_SPEC, ANY_SPEC] + [VMEM_SPEC] * 6,
        out_specs=VMEM_SPEC,
        compiler_params=pltpu.CompilerParams(vmem_limit_bytes=16 * MIB),
        cost_estimate=LIGHT,
        name="project_rest",
    )(weight, after, left, total, left_other, total_other, cosine, sine)


def small_call(kernel, out_shape, *args, in_specs=None):
    return pl.pallas_call(
        kernel,
        out_shape=out_shape,
        in_specs=in_specs or [VMEM_SPEC] * len(args),
        out_specs=jax.tree.map(lambda _: VMEM_SPEC, out_shape),
        compiler_params=pltpu.CompilerParams(vmem_limit_bytes=8 * MIB),
        cost_estimate=LIGHT,
        name="small",
    )(*args)


def angles_kernel(start, frequency, cosine, sine):
    rows = cosine.shape[1]
    chip = lax.div(lax.axis_index("gy"), 2)
    column = lax.broadcasted_iota(jnp.int32, (HD // 2, rows), 1)
    positions = (start[0] + chip * rows + column).astype(jnp.float32)
    angles = positions * frequency[...]
    cos, sin = jnp.cos(angles), jnp.sin(angles)
    cosine[0 : HD // 2, :] = cos
    cosine[HD // 2 : HD, :] = cos
    sine[0 : HD // 2, :] = -sin
    sine[HD // 2 : HD, :] = sin


def angles_of(start, rows):
    frequency = 10000.0 ** (-2.0 * np.arange(HD // 2) / HD)
    frequency = jnp.asarray(np.repeat(frequency[:, None], rows, axis=1), jnp.float32)
    shape = jax.ShapeDtypeStruct((HD, rows), jnp.float32)
    specs = [pl.BlockSpec(memory_space=pltpu.SMEM), VMEM_SPEC]
    return small_call(angles_kernel, (shape, shape), start, frequency, in_specs=specs)


def beside_kernel(left, right, out):
    columns = left.shape[1]
    out[:, 0:columns] = left[...]
    out[:, columns : 2 * columns] = right[...]


def beside(left, right):
    rows, columns = left.shape
    shape = jax.ShapeDtypeStruct((rows, 2 * columns), left.dtype)
    return small_call(beside_kernel, shape, left, right)


def halves_kernel(first, second, low, high):
    columns = low.shape[1]
    low[...] = first[:, 0:columns]
    high[...] = second[:, columns : 2 * columns]


def halves(first, second):
    rows, columns = first.shape
    shape = jax.ShapeDtypeStruct((rows, columns // 2), first.dtype)
    return small_call(halves_kernel, (shape, shape), first, second)


QB = 256


def window(q_ref, kv_ref, keys, i, low):
    count = q_ref.shape[1] // QB
    first, last = (0, i + 1) if low else (i, count)
    at = pl.ds(i * QB, QB)
    query = jnp.concatenate([q_ref[0:HD, at], q_ref[HD : 2 * HD, at]], axis=1)
    total, weight = None, None
    for j in range(first, last):
        here = slice(j * QB, (j + 1) * QB)
        e = jnp.exp(jnp.dot(keys[here], query, preferred_element_type=jnp.float32))
        if j == i:
            key = lax.broadcasted_iota(jnp.int32, (QB, QB), 0)
            column = lax.broadcasted_iota(jnp.int32, (QB, QB), 1)
            keep = key <= column if low else key > column
            e = jnp.where(jnp.concatenate([keep, keep], axis=1), e, 0.0)
        w = jnp.sum(e, axis=0, keepdims=True)
        t = jnp.dot(
            kv_ref[HD : 2 * HD, here], e.astype(jnp.bfloat16), preferred_element_type=jnp.float32
        )
        total = t if total is None else total + t
        weight = w if weight is None else weight + w
    return total, weight


def own_kernel(q_ref, kv_ref, total_ref, weight_ref, keys):
    keys[...] = kv_ref[0:HD, :].T
    for i in range(q_ref.shape[1] // QB):
        total, weight = window(q_ref, kv_ref, keys, i, True)
        for h in range(2):
            part = slice(h * QB, (h + 1) * QB)
            at = pl.ds(i * QB, QB)
            total_ref[h * HD : (h + 1) * HD, at] = total[:, part]
            weight_ref[h : h + 1, at] = weight[:, part]


def before_kernel(q_ref, sent_ref, cached_ref, total_ref, weight_ref, mixed_ref, kv_ref, keys):
    chip = lax.div(lax.axis_index("gy"), 2)

    @pl.when(chip == 0)
    def _():
        kv_ref[...] = cached_ref[...]

    @pl.when(chip > 0)
    def _():
        kv_ref[...] = sent_ref[...]

    keys[...] = kv_ref[0:HD, :].T
    for i in range(q_ref.shape[1] // QB):
        total, weight = window(q_ref, kv_ref, keys, i, False)
        for h in range(2):
            part = slice(h * QB, (h + 1) * QB)
            at = pl.ds(i * QB, QB)
            row = slice(h * HD, (h + 1) * HD)
            top = total[:, part] + total_ref[row, at]
            low = weight[:, part] + weight_ref[h : h + 1, at]
            mixed_ref[row, at] = (top / low).astype(jnp.bfloat16)


def attend_own(q, kv):
    rows = q.shape[1]
    return pl.pallas_call(
        own_kernel,
        out_shape=(
            jax.ShapeDtypeStruct(q.shape, jnp.float32),
            jax.ShapeDtypeStruct((2, rows), jnp.float32),
        ),
        scratch_shapes=[pltpu.VMEM((rows, HD), jnp.bfloat16)],
        compiler_params=pltpu.CompilerParams(vmem_limit_bytes=20 * MIB),
        cost_estimate=LIGHT,
        name="attend_own",
    )(q, kv)


def attend_before(q, sent, cached, total, weight):
    rows = q.shape[1]
    return pl.pallas_call(
        before_kernel,
        out_shape=jax.ShapeDtypeStruct(q.shape, jnp.bfloat16),
        scratch_shapes=[
            pltpu.VMEM(sent.shape, jnp.bfloat16),
            pltpu.VMEM((rows, HD), jnp.bfloat16),
        ],
        compiler_params=pltpu.CompilerParams(vmem_limit_bytes=20 * MIB),
        cost_estimate=LIGHT,
        name="attend_before",
    )(q, sent, cached, total, weight)


def out_most_kernel(*refs):
    mixed, weights = refs[0:7], refs[7:15]
    total, left, held_m, held_w, sems = refs[15:]
    depth = mixed[0].shape[0]
    slots = out_slots()
    copies = []
    for i in range(8):
        to = held_w.at[:, pl.ds(pl.multiple_of(slots[i] * depth, depth), depth)]
        copies.append(pltpu.make_async_copy(weights[i], to, sems.at[8 + i]))
    for i in range(7):
        here = held_m.at[pl.ds(i * depth, depth), :]
        copies.append(pltpu.make_async_copy(mixed[i], here, sems.at[i]))
    for copy in copies:
        copy.start()
    for copy in copies:
        copy.wait()
    rows = total.shape[2]
    left[...] = held_w[:, 7 * depth : 8 * depth]
    for half in range(2):
        here = held_m[:, half * rows : (half + 1) * rows]
        total[half] = jnp.dot(
            held_w[:, 0 : 7 * depth], here, preferred_element_type=jnp.float32
        )


def out_rest_kernel(flip, left, low, high, total, out):
    core = lax.rem(lax.axis_index("gy"), 2)
    half = 1 - core if flip else core
    for side, mixed in enumerate((low, high)):

        @pl.when(half == side)
        def _():
            product = jnp.dot(left[...], mixed[...], preferred_element_type=jnp.float32)
            out[...] = (total[side] + product).astype(out.dtype)


def out_most(mixed, weights):
    width, depth = weights[0].shape
    rows = mixed[0].shape[1] // 2
    return pl.pallas_call(
        out_most_kernel,
        out_shape=(
            jax.ShapeDtypeStruct((2, width, rows), jnp.float32),
            jax.ShapeDtypeStruct((width, depth), jnp.bfloat16),
        ),
        in_specs=[ANY_SPEC] * 15,
        out_specs=(VMEM_SPEC, VMEM_SPEC),
        scratch_shapes=[
            pltpu.VMEM((7 * depth, 2 * rows), jnp.bfloat16),
            pltpu.VMEM((width, 8 * depth), jnp.bfloat16),
            pltpu.SemaphoreType.DMA((16,)),
        ],
        compiler_params=pltpu.CompilerParams(vmem_limit_bytes=20 * MIB),
        cost_estimate=LIGHT,
        name="out_most",
    )(*mixed, *weights)


def out_rest(left, low, high, total, kind, flip):
    return pl.pallas_call(
        functools.partial(out_rest_kernel, flip),
        out_shape=jax.ShapeDtypeStruct(total.shape[1:], kind),
        in_specs=[VMEM_SPEC] * 4,
        out_specs=VMEM_SPEC,
        compiler_params=pltpu.CompilerParams(vmem_limit_bytes=20 * MIB),
        cost_estimate=LIGHT,
        name="out_rest",
    )(left, low, high, total)


def shards(hidden, start, w_query, w_key_value, w_out, cache):
    rows, width = hidden.shape
    kv_weight = w_key_value.reshape(width, 2 * HD)
    kv_weight, hidden = together(kv_weight, hidden)
    block = hidden.T
    out_block = w_out.T

    moved_q, moved_kv = shear_y(w_query), shear_y(kv_weight)
    block_z = swap_zh(block)
    block_r, block_l = shift_x(block, 1), shift_x(block, -1)
    moved_q, moved_kv, block_z, block_r, block_l, out_block, cache = together(
        moved_q, moved_kv, block_z, block_r, block_l, out_block, cache
    )
    moved = turn_x(beside(moved_kv, moved_q))
    out_z, out_r, out_l = swap_zl(out_block), shift_y(out_block, 1), shift_y(out_block, -1)
    other = [swap_core(block), swap_core(block_z)]
    cosine, sine = angles_of(start, 2 * rows)
    moved, block_z, block_r, block_l, out_z, out_r, out_l, cosine, sine, *other = together(
        moved, block_z, block_r, block_l, out_z, out_r, out_l, cosine, sine, *other
    )
    moved_z = swap_zl(moved)
    moved_r, moved_l = shift_y(moved, 1), shift_y(moved, -1)
    block_zr, block_zl = shift_x(block_z, 1), shift_x(block_z, -1)
    moved_z, moved_r, moved_l, block_zr, block_zl, block_r, block_l = together(
        moved_z, moved_r, moved_l, block_zr, block_zl, block_r, block_l
    )
    moved_f, moved_zl, moved_zr = shift_y(moved_r, 1), shift_y(moved_z, -1), swap_zl(moved_r)
    block_f, block_zf = shift_x(block_r, 1), shift_x(block_zl, -1)
    early = turn([moved, moved_z, moved_r, moved_l])
    moved_f, moved_zr, moved_zl, block_f, block_zf, cache, early = together(
        moved_f, moved_zr, moved_zl, block_f, block_zf, cache, early
    )
    half_zl, half_zr = halves(moved_zl, moved_zr)
    last_kv, last_q = shift_y(half_zl, -1), shift_y(half_zr, 1)
    late = turn([moved_zr, moved_zl, moved_f])
    own = [block, block_z, block_r, block_l, block_zr, block_zl, block_f, block_zf]
    other += [swap_core(b) for b in (block_r, block_l, block_zr, block_zl, block_f, block_zf)]
    pairs = []
    for gx in range(8):
        head = 8 * (gx % 2) + 2 * (gx // 2)
        pairs += [(gx * 16 + head + c, gx * 16 + c) for c in range(2)]
    cached = lax.ppermute(cache, AXES, pairs)
    most = project_most(own, early, late)
    most_other = project_most(other, early, late)
    kv = project_rest(project_kv_kernel, last_kv, last_q, most, most_other, cosine, sine)
    before = lax.ppermute(kv, "gy", [(i, i + 2) for i in range(14)])
    q = project_rest(project_q_kernel, last_q, kv, most, most_other, cosine, sine)

    kv, q, out_z, out_l = together(kv, q, out_z, out_l)
    out_f, out_zl = shift_y(out_l, -1), shift_y(out_z, -1)
    total, weight_sum = attend_own(q, kv)
    total, weight_sum, cached = together(total, weight_sum, cached)
    cached = cached.reshape(2 * rows, 2 * HD).T
    mixed = attend_before(q, before, cached, total, weight_sum)

    mixed, out_z, out_zl = together(mixed, out_z, out_zl)
    mixed_z = swap_zh(mixed)
    mixed_r, mixed_l = shift_x(mixed, 1), shift_x(mixed, -1)
    out_zr, out_zf = shift_y(out_z, 1), shift_y(out_zl, -1)
    mixed_z, mixed_r, mixed_l, out_zr, out_zf = together(mixed_z, mixed_r, mixed_l, out_zr, out_zf)
    mixed_f, mixed_zl, mixed_zr = shift_x(mixed_r, 1), shift_x(mixed_z, -1), swap_zh(mixed_r)
    mixed_f, mixed_zr, mixed_zl = together(mixed_f, mixed_zr, mixed_zl)
    low, high = halves(mixed_zr, mixed_zl)
    low, high = shift_x(low, 1), shift_x(high, -1)
    outs = [out_block, out_z, out_r, out_l, out_zr, out_zl, out_f, out_zf]
    gathered = [mixed, mixed_z, mixed_r, mixed_l, mixed_zr, mixed_zl, mixed_f]
    total, left = out_most(gathered, outs)
    sent = swap_core(out_rest(left, low, high, total, jnp.bfloat16, True))
    kept = out_rest(left, low, high, total, jnp.float32, False)
    return (kept + sent.astype(jnp.float32)).astype(jnp.bfloat16).T


def solution(mesh):
    return jax.shard_map(
        shards,
        mesh=mesh,
        in_specs=(
            P("gy", "gx"),
            P(),
            P("gx", "gy"),
            P("gx", None, "gy"),
            P("gy", "gx"),
            P(None, None, "gy"),
        ),
        out_specs=P("gy", "gx"),
        check_vma=False,
    )
```

```python
import functools

import jax
import jax.numpy as jnp
import numpy as np
from jax import lax
from jax.experimental import pallas as pl
from jax.experimental.pallas import tpu as pltpu
from jax.sharding import PartitionSpec as P

HD = 128
AXES = ("gx", "gy")
MIB = 1024 * 1024

query_scale = 168.0 ** (-0.5)
norm_eps = 1e-06


def place(index):
    gx, gy = divmod(index, 16)
    x, zh = divmod(gx, 2)
    zl, rest = divmod(gy, 8)
    y, core = divmod(rest, 2)
    return x, zh, zl, y, core


def number(x, zh, zl, y, core):
    return ((x % 4) * 2 + zh) * 16 + zl * 8 + (y % 4) * 2 + core


def move(value, to):
    return lax.ppermute(value, AXES, [(i, number(*to(*place(i)))) for i in range(128)])


def shift_x(value, by):
    return move(value, lambda x, zh, zl, y, c: (x + by, zh, zl, y, c))


def shift_y(value, by):
    return move(value, lambda x, zh, zl, y, c: (x, zh, zl, y + by, c))


def swap_zh(value):
    return move(value, lambda x, zh, zl, y, c: (x, 1 - zh, zl, y, c))


def swap_zl(value):
    return move(value, lambda x, zh, zl, y, c: (x, zh, 1 - zl, y, c))


def swap_core(value):
    return move(value, lambda x, zh, zl, y, c: (x, zh, zl, y, 1 - c))


def shear_y(value):
    return move(value, lambda x, zh, zl, y, c: (x, zh, zl, y + x, c))


def turn_x(value):
    return move(value, lambda x, zh, zl, y, c: (y - x, zl, zh, y, c))


def together(*values):
    return lax.optimization_barrier(values)


OFFSETS = ((0, 0), (0, 1), (3, 0), (1, 0), (3, 1), (1, 1), (2, 0), (2, 1))


def index_of(ring, pair):
    ring, pair = lax.rem(ring + 8, 4), lax.rem(pair, 2)
    base = jnp.where(ring == 0, 0, jnp.where(ring == 3, 2, jnp.where(ring == 1, 3, 6)))
    step = jnp.where((ring == 0) | (ring == 2), 1, 2)
    return base + step * pair


def coordinates():
    gx, gy = lax.axis_index("gx"), lax.axis_index("gy")
    zl, rest = lax.div(gy, 8), lax.rem(gy, 8)
    return lax.div(gx, 2), lax.rem(gx, 2), zl, lax.div(rest, 2), lax.rem(rest, 2)


def out_slots():
    x, zh, zl, y, core = coordinates()
    return [index_of(y + d - x, zl + e + zh) for d, e in OFFSETS]


def hidden_slots():
    x, zh, zl, y, core = coordinates()
    return [index_of(2 * x + d - y, zh + e + zl) for d, e in OFFSETS]


def turn_kernel(*refs):
    blocks, out = refs[:-1], refs[-1]
    for i, block in enumerate(blocks):
        out[i] = block[...].T


def turn(blocks):
    width, columns = blocks[0].shape
    shape = jax.ShapeDtypeStruct((len(blocks), columns, width), blocks[0].dtype)
    return small_call(turn_kernel, shape, *blocks)


def project_most_kernel(*refs):
    blocks, early, late, total, left = refs[0:8], refs[8], refs[9], refs[10], refs[11]
    slots = hidden_slots()
    total[...] = jnp.zeros_like(total)
    for j in range(8):

        @pl.when(slots[j] < 4)
        def _():
            weight = early[jnp.minimum(slots[j], 3)]
            total[...] += jnp.dot(weight, blocks[j][...], preferred_element_type=jnp.float32)

        @pl.when((slots[j] >= 4) & (slots[j] < 7))
        def _():
            weight = late[jnp.clip(slots[j] - 4, 0, 2)]
            total[...] += jnp.dot(weight, blocks[j][...], preferred_element_type=jnp.float32)

        @pl.when(slots[j] == 7)
        def _():
            left[...] = blocks[j][...]


def turned(v, cos, sin):
    v = v * lax.rsqrt(jnp.mean(v * v, axis=0, keepdims=True) + norm_eps)
    swapped = jnp.concatenate([v[HD // 2 :], v[: HD // 2]], axis=0)
    return v * cos + swapped * sin


def places(rows):
    core = lax.rem(lax.axis_index("gy"), 2)
    for half in (core, 1 - core):
        yield pl.ds(pl.multiple_of(half * rows, rows), rows)


def project_kv_kernel(weight, q_weight, *refs):
    (left, before), (left_other, before_other), (cosine, sine, kv_out) = refs[0:2], refs[2:4], refs[4:]
    turned_weight = weight[...].T
    halves = ((left, before), (left_other, before_other))
    for (block, total), at in zip(halves, places(left.shape[1])):
        product = jnp.dot(turned_weight, block[...], preferred_element_type=jnp.float32)
        values = (total[0 : 2 * HD, :] + product).astype(jnp.bfloat16)
        key = turned(values[0:HD].astype(jnp.float32), cosine[:, at], sine[:, at])
        kv_out[0:HD, at] = key.astype(jnp.bfloat16)
        kv_out[HD : 2 * HD, at] = values[HD : 2 * HD]


def project_q_kernel(weight, kv, *refs):
    (left, before), (left_other, before_other), (cosine, sine, q_out) = refs[0:2], refs[2:4], refs[4:]
    turned_weight = weight[...].T
    halves = ((left, before), (left_other, before_other))
    for (block, total), at in zip(halves, places(left.shape[1])):
        product = jnp.dot(turned_weight, block[...], preferred_element_type=jnp.float32)
        values = (total[2 * HD : 4 * HD, :] + product).astype(jnp.bfloat16).astype(jnp.float32)
        for h in range(2):
            part = slice(h * HD, (h + 1) * HD)
            query = turned(values[part], cosine[:, at], sine[:, at]) * query_scale
            q_out[part, at] = query.astype(jnp.bfloat16)


LIGHT = pl.CostEstimate(flops=1024, bytes_accessed=1024, transcendentals=0)
ANY_SPEC = pl.BlockSpec(memory_space=pl.ANY)
VMEM_SPEC = pl.BlockSpec(memory_space=pltpu.VMEM)


def project_most(blocks, early, late):
    width, rows = blocks[0].shape
    columns = early.shape[1]
    return pl.pallas_call(
        project_most_kernel,
        out_shape=(
            jax.ShapeDtypeStruct((columns, rows), jnp.float32),
            jax.ShapeDtypeStruct((width, rows), jnp.bfloat16),
        ),
        in_specs=[VMEM_SPEC] * 10,
        out_specs=(VMEM_SPEC, VMEM_SPEC),
        compiler_params=pltpu.CompilerParams(vmem_limit_bytes=20 * MIB),
        cost_estimate=pl.CostEstimate(
            flops=14 * rows * width * columns, bytes_accessed=15 * MIB, transcendentals=0
        ),
        name="project_most",
    )(*blocks, early, late)


def project_rest(kernel, weight, after, most, most_other, cosine, sine):
    (total, left), (total_other, left_other) = most, most_other
    return pl.pallas_call(
        kernel,
        out_shape=jax.ShapeDtypeStruct((weight.shape[1], 2 * left.shape[1]), jnp.bfloat16),
        in_specs=[VMEM_SPEC, ANY_SPEC] + [VMEM_SPEC] * 6,
        out_specs=VMEM_SPEC,
        compiler_params=pltpu.CompilerParams(vmem_limit_bytes=16 * MIB),
        cost_estimate=LIGHT,
        name="project_rest",
    )(weight, after, left, total, left_other, total_other, cosine, sine)


def small_call(kernel, out_shape, *args, in_specs=None):
    return pl.pallas_call(
        kernel,
        out_shape=out_shape,
        in_specs=in_specs or [VMEM_SPEC] * len(args),
        out_specs=jax.tree.map(lambda _: VMEM_SPEC, out_shape),
        compiler_params=pltpu.CompilerParams(vmem_limit_bytes=8 * MIB),
        cost_estimate=LIGHT,
        name="small",
    )(*args)


def angles_kernel(start, frequency, cosine, sine):
    rows = cosine.shape[1]
    chip = lax.div(lax.axis_index("gy"), 2)
    column = lax.broadcasted_iota(jnp.int32, (HD // 2, rows), 1)
    positions = (start[0] + chip * rows + column).astype(jnp.float32)
    angles = positions * frequency[...]
    cos, sin = jnp.cos(angles), jnp.sin(angles)
    cosine[0 : HD // 2, :] = cos
    cosine[HD // 2 : HD, :] = cos
    sine[0 : HD // 2, :] = -sin
    sine[HD // 2 : HD, :] = sin


def angles_of(start, rows):
    frequency = 10000.0 ** (-2.0 * np.arange(HD // 2) / HD)
    frequency = jnp.asarray(np.repeat(frequency[:, None], rows, axis=1), jnp.float32)
    shape = jax.ShapeDtypeStruct((HD, rows), jnp.float32)
    specs = [pl.BlockSpec(memory_space=pltpu.SMEM), VMEM_SPEC]
    return small_call(angles_kernel, (shape, shape), start, frequency, in_specs=specs)


def beside_kernel(left, right, out):
    columns = left.shape[1]
    out[:, 0:columns] = left[...]
    out[:, columns : 2 * columns] = right[...]


def beside(left, right):
    rows, columns = left.shape
    shape = jax.ShapeDtypeStruct((rows, 2 * columns), left.dtype)
    return small_call(beside_kernel, shape, left, right)


def halves_kernel(first, second, low, high):
    columns = low.shape[1]
    low[...] = first[:, 0:columns]
    high[...] = second[:, columns : 2 * columns]


def halves(first, second):
    rows, columns = first.shape
    shape = jax.ShapeDtypeStruct((rows, columns // 2), first.dtype)
    return small_call(halves_kernel, (shape, shape), first, second)


QB = 256


def window(q_ref, kv_ref, keys, i, low):
    count = q_ref.shape[1] // QB
    first, last = (0, i + 1) if low else (i, count)
    at = pl.ds(i * QB, QB)
    query = jnp.concatenate([q_ref[0:HD, at], q_ref[HD : 2 * HD, at]], axis=1)
    total, weight = None, None
    for j in range(first, last):
        here = slice(j * QB, (j + 1) * QB)
        e = jnp.exp(jnp.dot(keys[here], query, preferred_element_type=jnp.float32))
        if j == i:
            key = lax.broadcasted_iota(jnp.int32, (QB, QB), 0)
            column = lax.broadcasted_iota(jnp.int32, (QB, QB), 1)
            keep = key <= column if low else key > column
            e = jnp.where(jnp.concatenate([keep, keep], axis=1), e, 0.0)
        w = jnp.sum(e, axis=0, keepdims=True)
        t = jnp.dot(
            kv_ref[HD : 2 * HD, here], e.astype(jnp.bfloat16), preferred_element_type=jnp.float32
        )
        total = t if total is None else total + t
        weight = w if weight is None else weight + w
    return total, weight


def own_kernel(q_ref, kv_ref, total_ref, weight_ref, keys):
    keys[...] = kv_ref[0:HD, :].T
    for i in range(q_ref.shape[1] // QB):
        total, weight = window(q_ref, kv_ref, keys, i, True)
        for h in range(2):
            part = slice(h * QB, (h + 1) * QB)
            at = pl.ds(i * QB, QB)
            total_ref[h * HD : (h + 1) * HD, at] = total[:, part]
            weight_ref[h : h + 1, at] = weight[:, part]


def before_kernel(q_ref, sent_ref, cached_ref, total_ref, weight_ref, mixed_ref, kv_ref, keys):
    chip = lax.div(lax.axis_index("gy"), 2)

    @pl.when(chip == 0)
    def _():
        kv_ref[...] = cached_ref[...]

    @pl.when(chip > 0)
    def _():
        kv_ref[...] = sent_ref[...]

    keys[...] = kv_ref[0:HD, :].T
    for i in range(q_ref.shape[1] // QB):
        total, weight = window(q_ref, kv_ref, keys, i, False)
        for h in range(2):
            part = slice(h * QB, (h + 1) * QB)
            at = pl.ds(i * QB, QB)
            row = slice(h * HD, (h + 1) * HD)
            top = total[:, part] + total_ref[row, at]
            low = weight[:, part] + weight_ref[h : h + 1, at]
            mixed_ref[row, at] = (top / low).astype(jnp.bfloat16)


def attend_own(q, kv):
    rows = q.shape[1]
    return pl.pallas_call(
        own_kernel,
        out_shape=(
            jax.ShapeDtypeStruct(q.shape, jnp.float32),
            jax.ShapeDtypeStruct((2, rows), jnp.float32),
        ),
        scratch_shapes=[pltpu.VMEM((rows, HD), jnp.bfloat16)],
        compiler_params=pltpu.CompilerParams(vmem_limit_bytes=20 * MIB),
        cost_estimate=LIGHT,
        name="attend_own",
    )(q, kv)


def attend_before(q, sent, cached, total, weight):
    rows = q.shape[1]
    return pl.pallas_call(
        before_kernel,
        out_shape=jax.ShapeDtypeStruct(q.shape, jnp.bfloat16),
        scratch_shapes=[
            pltpu.VMEM(sent.shape, jnp.bfloat16),
            pltpu.VMEM((rows, HD), jnp.bfloat16),
        ],
        compiler_params=pltpu.CompilerParams(vmem_limit_bytes=20 * MIB),
        cost_estimate=LIGHT,
        name="attend_before",
    )(q, sent, cached, total, weight)


def out_most_kernel(*refs):
    mixed, weights = refs[0:7], refs[7:15]
    total, left, held_m, held_w, sems = refs[15:]
    depth = mixed[0].shape[0]
    slots = out_slots()
    copies = []
    for i in range(8):
        to = held_w.at[:, pl.ds(pl.multiple_of(slots[i] * depth, depth), depth)]
        copies.append(pltpu.make_async_copy(weights[i], to, sems.at[8 + i]))
    for i in range(7):
        here = held_m.at[pl.ds(i * depth, depth), :]
        copies.append(pltpu.make_async_copy(mixed[i], here, sems.at[i]))
    for copy in copies:
        copy.start()
    for copy in copies:
        copy.wait()
    rows = total.shape[2]
    left[...] = held_w[:, 7 * depth : 8 * depth]
    for half in range(2):
        here = held_m[:, half * rows : (half + 1) * rows]
        total[half] = jnp.dot(
            held_w[:, 0 : 7 * depth], here, preferred_element_type=jnp.float32
        )


def out_rest_kernel(flip, left, low, high, total, out):
    core = lax.rem(lax.axis_index("gy"), 2)
    half = 1 - core if flip else core
    for side, mixed in enumerate((low, high)):

        @pl.when(half == side)
        def _():
            product = jnp.dot(left[...], mixed[...], preferred_element_type=jnp.float32)
            out[...] = (total[side] + product).astype(out.dtype)


def out_most(mixed, weights):
    width, depth = weights[0].shape
    rows = mixed[0].shape[1] // 2
    return pl.pallas_call(
        out_most_kernel,
        out_shape=(
            jax.ShapeDtypeStruct((2, width, rows), jnp.float32),
            jax.ShapeDtypeStruct((width, depth), jnp.bfloat16),
        ),
        in_specs=[ANY_SPEC] * 15,
        out_specs=(VMEM_SPEC, VMEM_SPEC),
        scratch_shapes=[
            pltpu.VMEM((7 * depth, 2 * rows), jnp.bfloat16),
            pltpu.VMEM((width, 8 * depth), jnp.bfloat16),
            pltpu.SemaphoreType.DMA((16,)),
        ],
        compiler_params=pltpu.CompilerParams(vmem_limit_bytes=20 * MIB),
        cost_estimate=LIGHT,
        name="out_most",
    )(*mixed, *weights)


def out_rest(left, low, high, total, kind, flip):
    return pl.pallas_call(
        functools.partial(out_rest_kernel, flip),
        out_shape=jax.ShapeDtypeStruct(total.shape[1:], kind),
        in_specs=[VMEM_SPEC] * 4,
        out_specs=VMEM_SPEC,
        compiler_params=pltpu.CompilerParams(vmem_limit_bytes=20 * MIB),
        cost_estimate=LIGHT,
        name="out_rest",
    )(left, low, high, total)


def shards(hidden, start, w_query, w_key_value, w_out, cache):
    rows, width = hidden.shape
    kv_weight = w_key_value.reshape(width, 2 * HD)
    kv_weight, hidden = together(kv_weight, hidden)
    block = hidden.T
    out_block = w_out.T

    moved = shear_y(beside(kv_weight, w_query))
    block_z = swap_zh(block)
    block_r, block_l = shift_x(block, 1), shift_x(block, -1)
    moved, block_z, block_r, block_l, out_block, cache = together(
        moved, block_z, block_r, block_l, out_block, cache
    )
    moved = turn_x(moved)
    out_z, out_r, out_l = swap_zl(out_block), shift_y(out_block, 1), shift_y(out_block, -1)
    other = [swap_core(block), swap_core(block_z)]
    cosine, sine = angles_of(start, 2 * rows)
    moved, block_z, block_r, block_l, out_z, out_r, out_l, cosine, sine, *other = together(
        moved, block_z, block_r, block_l, out_z, out_r, out_l, cosine, sine, *other
    )
    moved_z = swap_zl(moved)
    moved_r, moved_l = shift_y(moved, 1), shift_y(moved, -1)
    block_zr, block_zl = shift_x(block_z, 1), shift_x(block_z, -1)
    moved_z, moved_r, moved_l, block_zr, block_zl, block_r, block_l = together(
        moved_z, moved_r, moved_l, block_zr, block_zl, block_r, block_l
    )
    moved_f, moved_zl, moved_zr = shift_y(moved_r, 1), shift_y(moved_z, -1), swap_zl(moved_r)
    block_f, block_zf = shift_x(block_r, 1), shift_x(block_zl, -1)
    early = turn([moved, moved_z, moved_r, moved_l])
    moved_f, moved_zr, moved_zl, block_f, block_zf, cache, early = together(
        moved_f, moved_zr, moved_zl, block_f, block_zf, cache, early
    )
    half_zl, half_zr = halves(moved_zl, moved_zr)
    last_kv, last_q = shift_y(half_zl, -1), shift_y(half_zr, 1)
    late = turn([moved_zr, moved_zl, moved_f])
    own = [block, block_z, block_r, block_l, block_zr, block_zl, block_f, block_zf]
    other += [swap_core(b) for b in (block_r, block_l, block_zr, block_zl, block_f, block_zf)]
    pairs = []
    for gx in range(8):
        head = 8 * (gx % 2) + 2 * (gx // 2)
        pairs += [(gx * 16 + head + c, gx * 16 + c) for c in range(2)]
    cached = lax.ppermute(cache, AXES, pairs)
    most = project_most(own, early, late)
    most_other = project_most(other, early, late)
    kv = project_rest(project_kv_kernel, last_kv, last_q, most, most_other, cosine, sine)
    before = lax.ppermute(kv, "gy", [(i, i + 2) for i in range(14)])
    q = project_rest(project_q_kernel, last_q, kv, most, most_other, cosine, sine)

    kv, q, out_z, out_l = together(kv, q, out_z, out_l)
    out_f, out_zl = shift_y(out_l, -1), shift_y(out_z, -1)
    total, weight_sum = attend_own(q, kv)
    total, weight_sum, cached = together(total, weight_sum, cached)
    cached = cached.reshape(2 * rows, 2 * HD).T
    mixed = attend_before(q, before, cached, total, weight_sum)

    mixed, out_z, out_zl = together(mixed, out_z, out_zl)
    mixed_z = swap_zh(mixed)
    mixed_r, mixed_l = shift_x(mixed, 1), shift_x(mixed, -1)
    out_zr, out_zf = shift_y(out_z, 1), shift_y(out_zl, -1)
    mixed_z, mixed_r, mixed_l, out_zr, out_zf = together(mixed_z, mixed_r, mixed_l, out_zr, out_zf)
    mixed_f, mixed_zl, mixed_zr = shift_x(mixed_r, 1), shift_x(mixed_z, -1), swap_zh(mixed_r)
    mixed_f, mixed_zr, mixed_zl = together(mixed_f, mixed_zr, mixed_zl)
    low, high = halves(mixed_zr, mixed_zl)
    low, high = shift_x(low, 1), shift_x(high, -1)
    outs = [out_block, out_z, out_r, out_l, out_zr, out_zl, out_f, out_zf]
    gathered = [mixed, mixed_z, mixed_r, mixed_l, mixed_zr, mixed_zl, mixed_f]
    total, left = out_most(gathered, outs)
    sent = swap_core(out_rest(left, low, high, total, jnp.bfloat16, True))
    kept = out_rest(left, low, high, total, jnp.float32, False)
    return (kept + sent.astype(jnp.float32)).astype(jnp.bfloat16).T


def solution(mesh):
    return jax.shard_map(
        shards,
        mesh=mesh,
        in_specs=(
            P("gy", "gx"),
            P(),
            P("gx", "gy"),
            P("gx", None, "gy"),
            P("gy", "gx"),
            P(None, None, "gy"),
        ),
        out_specs=P("gy", "gx"),
        check_vma=False,
    )
```

```python
import functools

import jax
import jax.numpy as jnp
import numpy as np
from jax import lax
from jax.experimental import pallas as pl
from jax.experimental.pallas import tpu as pltpu
from jax.sharding import PartitionSpec as P

HD = 128
AXES = ("gx", "gy")
MIB = 1024 * 1024

query_scale = 168.0 ** (-0.5)
norm_eps = 1e-06


def place(index):
    gx, gy = divmod(index, 16)
    x, zh = divmod(gx, 2)
    zl, rest = divmod(gy, 8)
    y, core = divmod(rest, 2)
    return x, zh, zl, y, core


def number(x, zh, zl, y, core):
    return ((x % 4) * 2 + zh) * 16 + zl * 8 + (y % 4) * 2 + core


def move(value, to):
    return lax.ppermute(value, AXES, [(i, number(*to(*place(i)))) for i in range(128)])


def shift_x(value, by):
    return move(value, lambda x, zh, zl, y, c: (x + by, zh, zl, y, c))


def shift_y(value, by):
    return move(value, lambda x, zh, zl, y, c: (x, zh, zl, y + by, c))


def swap_zh(value):
    return move(value, lambda x, zh, zl, y, c: (x, 1 - zh, zl, y, c))


def swap_zl(value):
    return move(value, lambda x, zh, zl, y, c: (x, zh, 1 - zl, y, c))


def swap_core(value):
    return move(value, lambda x, zh, zl, y, c: (x, zh, zl, y, 1 - c))


def shear_y(value):
    return move(value, lambda x, zh, zl, y, c: (x, zh, zl, y + x, c))


def turn_x(value):
    return move(value, lambda x, zh, zl, y, c: (y - x, zl, zh, y, c))


def together(*values):
    return lax.optimization_barrier(values)


OFFSETS = ((0, 0), (0, 1), (3, 0), (1, 0), (3, 1), (1, 1), (2, 0), (2, 1))


def index_of(ring, pair):
    ring, pair = lax.rem(ring + 8, 4), lax.rem(pair, 2)
    base = jnp.where(ring == 0, 0, jnp.where(ring == 3, 2, jnp.where(ring == 1, 3, 6)))
    step = jnp.where((ring == 0) | (ring == 2), 1, 2)
    return base + step * pair


def coordinates():
    gx, gy = lax.axis_index("gx"), lax.axis_index("gy")
    zl, rest = lax.div(gy, 8), lax.rem(gy, 8)
    return lax.div(gx, 2), lax.rem(gx, 2), zl, lax.div(rest, 2), lax.rem(rest, 2)


def out_slots():
    x, zh, zl, y, core = coordinates()
    return [index_of(y + d - x, zl + e + zh) for d, e in OFFSETS]


def hidden_slots():
    x, zh, zl, y, core = coordinates()
    return [index_of(2 * x + d - y, zh + e + zl) for d, e in OFFSETS]


def turn_kernel(*refs):
    blocks, out = refs[:-1], refs[-1]
    for i, block in enumerate(blocks):
        out[i] = block[...].T


def turn(blocks):
    width, columns = blocks[0].shape
    shape = jax.ShapeDtypeStruct((len(blocks), columns, width), blocks[0].dtype)
    return small_call(turn_kernel, shape, *blocks)


def project_most_kernel(*refs):
    blocks, early, late, total, left = refs[0:8], refs[8], refs[9], refs[10], refs[11]
    slots = hidden_slots()
    total[...] = jnp.zeros_like(total)
    for j in range(8):

        @pl.when(slots[j] < 4)
        def _():
            weight = early[jnp.minimum(slots[j], 3)]
            total[...] += jnp.dot(weight, blocks[j][...], preferred_element_type=jnp.float32)

        @pl.when((slots[j] >= 4) & (slots[j] < 7))
        def _():
            weight = late[jnp.clip(slots[j] - 4, 0, 2)]
            total[...] += jnp.dot(weight, blocks[j][...], preferred_element_type=jnp.float32)

        @pl.when(slots[j] == 7)
        def _():
            left[...] = blocks[j][...]


def turned(v, cos, sin):
    v = v * lax.rsqrt(jnp.mean(v * v, axis=0, keepdims=True) + norm_eps)
    swapped = jnp.concatenate([v[HD // 2 :], v[: HD // 2]], axis=0)
    return v * cos + swapped * sin


def places(rows):
    core = lax.rem(lax.axis_index("gy"), 2)
    for half in (core, 1 - core):
        yield pl.ds(pl.multiple_of(half * rows, rows), rows)


def project_kv_kernel(weight, q_weight, *refs):
    (left, before), (left_other, before_other), (cosine, sine, kv_out) = refs[0:2], refs[2:4], refs[4:]
    turned_weight = weight[...].T
    halves = ((left, before), (left_other, before_other))
    for (block, total), at in zip(halves, places(left.shape[1])):
        product = jnp.dot(turned_weight, block[...], preferred_element_type=jnp.float32)
        values = (total[0 : 2 * HD, :] + product).astype(jnp.bfloat16)
        key = turned(values[0:HD].astype(jnp.float32), cosine[:, at], sine[:, at])
        kv_out[0:HD, at] = key.astype(jnp.bfloat16)
        kv_out[HD : 2 * HD, at] = values[HD : 2 * HD]


def project_q_kernel(weight, kv, *refs):
    (left, before), (left_other, before_other), (cosine, sine, q_out) = refs[0:2], refs[2:4], refs[4:]
    turned_weight = weight[...].T
    halves = ((left, before), (left_other, before_other))
    for (block, total), at in zip(halves, places(left.shape[1])):
        product = jnp.dot(turned_weight, block[...], preferred_element_type=jnp.float32)
        values = (total[2 * HD : 4 * HD, :] + product).astype(jnp.bfloat16).astype(jnp.float32)
        for h in range(2):
            part = slice(h * HD, (h + 1) * HD)
            query = turned(values[part], cosine[:, at], sine[:, at]) * query_scale
            q_out[part, at] = query.astype(jnp.bfloat16)


LIGHT = pl.CostEstimate(flops=1024, bytes_accessed=1024, transcendentals=0)
ANY_SPEC = pl.BlockSpec(memory_space=pl.ANY)
VMEM_SPEC = pl.BlockSpec(memory_space=pltpu.VMEM)


def project_most(blocks, early, late):
    width, rows = blocks[0].shape
    columns = early.shape[1]
    return pl.pallas_call(
        project_most_kernel,
        out_shape=(
            jax.ShapeDtypeStruct((columns, rows), jnp.float32),
            jax.ShapeDtypeStruct((width, rows), jnp.bfloat16),
        ),
        in_specs=[VMEM_SPEC] * 10,
        out_specs=(VMEM_SPEC, VMEM_SPEC),
        compiler_params=pltpu.CompilerParams(vmem_limit_bytes=20 * MIB),
        cost_estimate=pl.CostEstimate(
            flops=14 * rows * width * columns, bytes_accessed=15 * MIB, transcendentals=0
        ),
        name="project_most",
    )(*blocks, early, late)


def project_rest(kernel, weight, after, most, most_other, cosine, sine):
    (total, left), (total_other, left_other) = most, most_other
    return pl.pallas_call(
        kernel,
        out_shape=jax.ShapeDtypeStruct((weight.shape[1], 2 * left.shape[1]), jnp.bfloat16),
        in_specs=[VMEM_SPEC, ANY_SPEC] + [VMEM_SPEC] * 6,
        out_specs=VMEM_SPEC,
        compiler_params=pltpu.CompilerParams(vmem_limit_bytes=16 * MIB),
        cost_estimate=LIGHT,
        name="project_rest",
    )(weight, after, left, total, left_other, total_other, cosine, sine)


def small_call(kernel, out_shape, *args, in_specs=None):
    return pl.pallas_call(
        kernel,
        out_shape=out_shape,
        in_specs=in_specs or [VMEM_SPEC] * len(args),
        out_specs=jax.tree.map(lambda _: VMEM_SPEC, out_shape),
        compiler_params=pltpu.CompilerParams(vmem_limit_bytes=8 * MIB),
        cost_estimate=LIGHT,
        name="small",
    )(*args)


def angles_kernel(start, frequency, cosine, sine):
    rows = cosine.shape[1]
    chip = lax.div(lax.axis_index("gy"), 2)
    column = lax.broadcasted_iota(jnp.int32, (HD // 2, rows), 1)
    positions = (start[0] + chip * rows + column).astype(jnp.float32)
    angles = positions * frequency[...]
    cos, sin = jnp.cos(angles), jnp.sin(angles)
    cosine[0 : HD // 2, :] = cos
    cosine[HD // 2 : HD, :] = cos
    sine[0 : HD // 2, :] = -sin
    sine[HD // 2 : HD, :] = sin


def angles_of(start, rows):
    frequency = 10000.0 ** (-2.0 * np.arange(HD // 2) / HD)
    frequency = jnp.asarray(np.repeat(frequency[:, None], rows, axis=1), jnp.float32)
    shape = jax.ShapeDtypeStruct((HD, rows), jnp.float32)
    specs = [pl.BlockSpec(memory_space=pltpu.SMEM), VMEM_SPEC]
    return small_call(angles_kernel, (shape, shape), start, frequency, in_specs=specs)


def beside_kernel(left, right, out):
    columns = left.shape[1]
    out[:, 0:columns] = left[...]
    out[:, columns : 2 * columns] = right[...]


def beside(left, right):
    rows, columns = left.shape
    shape = jax.ShapeDtypeStruct((rows, 2 * columns), left.dtype)
    return small_call(beside_kernel, shape, left, right)


def halves_kernel(first, second, low, high):
    columns = low.shape[1]
    low[...] = first[:, 0:columns]
    high[...] = second[:, columns : 2 * columns]


def halves(first, second):
    rows, columns = first.shape
    shape = jax.ShapeDtypeStruct((rows, columns // 2), first.dtype)
    return small_call(halves_kernel, (shape, shape), first, second)


QB = 256


def window(q_ref, kv_ref, keys, i, low):
    count = q_ref.shape[1] // QB
    first, last = (0, i + 1) if low else (i, count)
    at = pl.ds(i * QB, QB)
    query = jnp.concatenate([q_ref[0:HD, at], q_ref[HD : 2 * HD, at]], axis=1)
    total, weight = None, None
    for j in range(first, last):
        here = slice(j * QB, (j + 1) * QB)
        e = jnp.exp(jnp.dot(keys[here], query, preferred_element_type=jnp.float32))
        if j == i:
            key = lax.broadcasted_iota(jnp.int32, (QB, QB), 0)
            column = lax.broadcasted_iota(jnp.int32, (QB, QB), 1)
            keep = key <= column if low else key > column
            e = jnp.where(jnp.concatenate([keep, keep], axis=1), e, 0.0)
        w = jnp.sum(e, axis=0, keepdims=True)
        t = jnp.dot(
            kv_ref[HD : 2 * HD, here], e.astype(jnp.bfloat16), preferred_element_type=jnp.float32
        )
        total = t if total is None else total + t
        weight = w if weight is None else weight + w
    return total, weight


def own_kernel(q_ref, kv_ref, total_ref, weight_ref, keys):
    keys[...] = kv_ref[0:HD, :].T
    for i in range(q_ref.shape[1] // QB):
        total, weight = window(q_ref, kv_ref, keys, i, True)
        for h in range(2):
            part = slice(h * QB, (h + 1) * QB)
            at = pl.ds(i * QB, QB)
            total_ref[h * HD : (h + 1) * HD, at] = total[:, part]
            weight_ref[h : h + 1, at] = weight[:, part]


def before_kernel(q_ref, sent_ref, cached_ref, total_ref, weight_ref, mixed_ref, kv_ref, keys):
    chip = lax.div(lax.axis_index("gy"), 2)

    @pl.when(chip == 0)
    def _():
        kv_ref[...] = cached_ref[...]

    @pl.when(chip > 0)
    def _():
        kv_ref[...] = sent_ref[...]

    keys[...] = kv_ref[0:HD, :].T
    for i in range(q_ref.shape[1] // QB):
        total, weight = window(q_ref, kv_ref, keys, i, False)
        for h in range(2):
            part = slice(h * QB, (h + 1) * QB)
            at = pl.ds(i * QB, QB)
            row = slice(h * HD, (h + 1) * HD)
            top = total[:, part] + total_ref[row, at]
            low = weight[:, part] + weight_ref[h : h + 1, at]
            mixed_ref[row, at] = (top / low).astype(jnp.bfloat16)


def attend_own(q, kv):
    rows = q.shape[1]
    return pl.pallas_call(
        own_kernel,
        out_shape=(
            jax.ShapeDtypeStruct(q.shape, jnp.float32),
            jax.ShapeDtypeStruct((2, rows), jnp.float32),
        ),
        scratch_shapes=[pltpu.VMEM((rows, HD), jnp.bfloat16)],
        compiler_params=pltpu.CompilerParams(vmem_limit_bytes=20 * MIB),
        cost_estimate=LIGHT,
        name="attend_own",
    )(q, kv)


def attend_before(q, sent, cached, total, weight):
    rows = q.shape[1]
    return pl.pallas_call(
        before_kernel,
        out_shape=jax.ShapeDtypeStruct(q.shape, jnp.bfloat16),
        scratch_shapes=[
            pltpu.VMEM(sent.shape, jnp.bfloat16),
            pltpu.VMEM((rows, HD), jnp.bfloat16),
        ],
        compiler_params=pltpu.CompilerParams(vmem_limit_bytes=20 * MIB),
        cost_estimate=LIGHT,
        name="attend_before",
    )(q, sent, cached, total, weight)


def out_most_kernel(*refs):
    mixed, weights = refs[0:7], refs[7:15]
    total, left, held_m, held_w, sems = refs[15:]
    depth = mixed[0].shape[0]
    slots = out_slots()
    copies = []
    for i in range(8):
        to = held_w.at[:, pl.ds(pl.multiple_of(slots[i] * depth, depth), depth)]
        copies.append(pltpu.make_async_copy(weights[i], to, sems.at[8 + i]))
    for i in range(7):
        here = held_m.at[pl.ds(i * depth, depth), :]
        copies.append(pltpu.make_async_copy(mixed[i], here, sems.at[i]))
    for copy in copies:
        copy.start()
    for copy in copies:
        copy.wait()
    rows = total.shape[2]
    left[...] = held_w[:, 7 * depth : 8 * depth]
    for half in range(2):
        here = held_m[:, half * rows : (half + 1) * rows]
        total[half] = jnp.dot(
            held_w[:, 0 : 7 * depth], here, preferred_element_type=jnp.float32
        )


def out_rest_kernel(flip, left, low, high, total, out):
    core = lax.rem(lax.axis_index("gy"), 2)
    half = 1 - core if flip else core
    for side, mixed in enumerate((low, high)):

        @pl.when(half == side)
        def _():
            product = jnp.dot(left[...], mixed[...], preferred_element_type=jnp.float32)
            out[...] = (total[side] + product).astype(out.dtype)


def out_most(mixed, weights):
    width, depth = weights[0].shape
    rows = mixed[0].shape[1] // 2
    return pl.pallas_call(
        out_most_kernel,
        out_shape=(
            jax.ShapeDtypeStruct((2, width, rows), jnp.float32),
            jax.ShapeDtypeStruct((width, depth), jnp.bfloat16),
        ),
        in_specs=[ANY_SPEC] * 15,
        out_specs=(VMEM_SPEC, VMEM_SPEC),
        scratch_shapes=[
            pltpu.VMEM((7 * depth, 2 * rows), jnp.bfloat16),
            pltpu.VMEM((width, 8 * depth), jnp.bfloat16),
            pltpu.SemaphoreType.DMA((16,)),
        ],
        compiler_params=pltpu.CompilerParams(vmem_limit_bytes=20 * MIB),
        cost_estimate=LIGHT,
        name="out_most",
    )(*mixed, *weights)


def out_rest(left, low, high, total, kind, flip):
    return pl.pallas_call(
        functools.partial(out_rest_kernel, flip),
        out_shape=jax.ShapeDtypeStruct(total.shape[1:], kind),
        in_specs=[VMEM_SPEC] * 4,
        out_specs=VMEM_SPEC,
        compiler_params=pltpu.CompilerParams(vmem_limit_bytes=20 * MIB),
        cost_estimate=LIGHT,
        name="out_rest",
    )(left, low, high, total)


def shards(hidden, start, w_query, w_key_value, w_out, cache):
    rows, width = hidden.shape
    kv_weight = w_key_value.reshape(width, 2 * HD)
    kv_weight, hidden = together(kv_weight, hidden)
    block = hidden.T
    out_block = w_out.T

    moved_q, moved_kv = shear_y(w_query), shear_y(kv_weight)
    block_z = swap_zh(block)
    block_r, block_l = shift_x(block, 1), shift_x(block, -1)
    moved_q, moved_kv, block_z, block_r, block_l, out_block, cache = together(
        moved_q, moved_kv, block_z, block_r, block_l, out_block, cache
    )
    moved = turn_x(beside(moved_kv, moved_q))
    out_z, out_r, out_l = swap_zl(out_block), shift_y(out_block, 1), shift_y(out_block, -1)
    other = [swap_core(block), swap_core(block_z), swap_core(block_r)]
    cosine, sine = angles_of(start, 2 * rows)
    moved, block_z, block_r, block_l, out_z, out_r, out_l, cosine, sine, *other = together(
        moved, block_z, block_r, block_l, out_z, out_r, out_l, cosine, sine, *other
    )
    moved_z = swap_zl(moved)
    moved_r, moved_l = shift_y(moved, 1), shift_y(moved, -1)
    block_zr, block_zl = shift_x(block_z, 1), shift_x(block_z, -1)
    moved_z, moved_r, moved_l, block_zr, block_zl, block_r, block_l = together(
        moved_z, moved_r, moved_l, block_zr, block_zl, block_r, block_l
    )
    moved_f, moved_zl, moved_zr = shift_y(moved_r, 1), shift_y(moved_z, -1), swap_zl(moved_r)
    block_f, block_zf = shift_x(block_r, 1), shift_x(block_zl, -1)
    early = turn([moved, moved_z, moved_r, moved_l])
    moved_f, moved_zr, moved_zl, block_f, block_zf, cache, early = together(
        moved_f, moved_zr, moved_zl, block_f, block_zf, cache, early
    )
    half_zl, half_zr = halves(moved_zl, moved_zr)
    last_kv, last_q = shift_y(half_zl, -1), shift_y(half_zr, 1)
    late = turn([moved_zr, moved_zl, moved_f])
    own = [block, block_z, block_r, block_l, block_zr, block_zl, block_f, block_zf]
    other += [swap_core(b) for b in (block_l, block_zr, block_zl, block_f, block_zf)]
    pairs = []
    for gx in range(8):
        head = 8 * (gx % 2) + 2 * (gx // 2)
        pairs += [(gx * 16 + head + c, gx * 16 + c) for c in range(2)]
    cached = lax.ppermute(cache, AXES, pairs)
    most = project_most(own, early, late)
    most_other = project_most(other, early, late)
    kv = project_rest(project_kv_kernel, last_kv, last_q, most, most_other, cosine, sine)
    before = lax.ppermute(kv, "gy", [(i, i + 2) for i in range(14)])
    q = project_rest(project_q_kernel, last_q, kv, most, most_other, cosine, sine)

    kv, q, out_z, out_l = together(kv, q, out_z, out_l)
    out_f, out_zl = shift_y(out_l, -1), shift_y(out_z, -1)
    total, weight_sum = attend_own(q, kv)
    total, weight_sum, cached = together(total, weight_sum, cached)
    cached = cached.reshape(2 * rows, 2 * HD).T
    mixed = attend_before(q, before, cached, total, weight_sum)

    mixed, out_z, out_zl = together(mixed, out_z, out_zl)
    mixed_z = swap_zh(mixed)
    mixed_r, mixed_l = shift_x(mixed, 1), shift_x(mixed, -1)
    out_zr, out_zf = shift_y(out_z, 1), shift_y(out_zl, -1)
    mixed_z, mixed_r, mixed_l, out_zr, out_zf = together(mixed_z, mixed_r, mixed_l, out_zr, out_zf)
    mixed_f, mixed_zl, mixed_zr = shift_x(mixed_r, 1), shift_x(mixed_z, -1), swap_zh(mixed_r)
    mixed_f, mixed_zr, mixed_zl = together(mixed_f, mixed_zr, mixed_zl)
    low, high = halves(mixed_zr, mixed_zl)
    low, high = shift_x(low, 1), shift_x(high, -1)
    outs = [out_block, out_z, out_r, out_l, out_zr, out_zl, out_f, out_zf]
    gathered = [mixed, mixed_z, mixed_r, mixed_l, mixed_zr, mixed_zl, mixed_f]
    total, left = out_most(gathered, outs)
    sent = swap_core(out_rest(left, low, high, total, jnp.bfloat16, True))
    kept = out_rest(left, low, high, total, jnp.float32, False)
    return (kept + sent.astype(jnp.float32)).astype(jnp.bfloat16).T


def solution(mesh):
    return jax.shard_map(
        shards,
        mesh=mesh,
        in_specs=(
            P("gy", "gx"),
            P(),
            P("gx", "gy"),
            P("gx", None, "gy"),
            P("gy", "gx"),
            P(None, None, "gy"),
        ),
        out_specs=P("gy", "gx"),
        check_vma=False,
    )
```
